32 devices in a mesh: groups: 2 (over y), tensor: 4 (over z), width: 4 (over x, core).
Axes of the slice: x: 2, y: 2, z: 4, core: 2. Of those that a mesh axis runs over, the one named last changes fastest.
Arguments:
- tokens: bfloat16 [1024, 8192], P(('groups', 'tensor'), 'width'), parts along dimension 0, may hold values from -60 to 60
- gate_weight: bfloat16 [8192, 14336], P('width', 'tensor'), may hold values from -0.0625 to 0.0625
- up_weight: bfloat16 [8192, 14336], P('width', 'tensor'), may hold values from -0.0625 to 0.0625
- down_weight: bfloat16 [14336, 8192], P('tensor', 'width'), may hold values from -0.046875 to 0.046875
Outputs:
- scaled_output: bfloat16 [1024, 8192], P(('groups', 'tensor'), 'width'), parts along dimension 0
- column_scales: float32 [16384], P(('groups', 'width')), parts along dimension 0
The draws below stay inside these ranges and needn't reach their ends.
There are 2 independent parts, one for each index of `groups`. The reference program is written for one: setup_inputs(seed, part) draws one part's arguments, and reference() takes and returns one part's arrays. A program takes and returns all parts, laid end to end along the dimension named above; an argument that names none is the same for every part. Nothing has to cross between parts.
All inputs are finite; a program needn't handle non-finite values. Where the reference program divides by a largest or mean magnitude, that divisor is 1e-20 or more.
Results may differ from the reference program's by a relative error of at most 0.022.
Values may be sent and summed in bfloat16 or wider, within the bound.
No kernel may reach another device: no remote copies, remote signals or barrier semaphores. Data moves between devices by JAX's collectives and lax.ppermute only.
A program may use at most 128 MiB of HBM per device.

```python
import math
import jax
import jax.numpy as jnp
from jax import lax

D = 8192
FF = 14336
TOKENS = 512
N_WIDTH = 4


def draw_tokens(key, part):
    key = jax.random.fold_in(key, 11)
    first, second, third = jax.random.split(key, 3)
    cols = jnp.exp(jax.random.uniform(first, (1, D), jnp.float32, math.log(0.3), math.log(3.0)))
    rows = jnp.exp(jax.random.uniform(second, (TOKENS, 1), jnp.float32, math.log(0.8), math.log(1.25)))
    base = jnp.clip(jax.random.normal(third, (TOKENS, D), jnp.float32), -6.0, 6.0)
    return (base * rows * cols).astype(jnp.bfloat16)


def levels(key, dims, shards, low, high):
    def one(position, shards_of):
        heights = jax.random.uniform(jax.random.fold_in(jax.random.fold_in(key, 6), position), (shards_of,), jnp.float32, low / len(shards), high / len(shards))
        return jnp.repeat(jnp.exp(heights), dims[position] // shards_of).reshape((-1,) + (1,) * (len(dims) - position - 1))

    level = one(*shards[0])
    for cut in shards[1:]:
        level = level * one(*cut)
    return level


def noise(key, extent, spread, reach, pieces=(), held_as=jnp.bfloat16):
    values = jax.random.normal(key, extent, jnp.float32) * spread
    if len(pieces) > 0:
        values = levels(key, extent, pieces, -0.22, 0.18) * values
    return jnp.clip(values, min=-reach, max=reach).astype(held_as)


def setup_inputs(seed: int = 0, part: int = 0) -> dict:
    arg_keys = jax.random.split(jax.random.key(seed), 5)
    part_keys = jax.random.split(jax.random.fold_in(arg_keys[4], part), 5)
    tokens = draw_tokens(jax.random.fold_in(jax.random.fold_in(arg_keys[4], part), 71), part)
    gate_weight = noise(arg_keys[1], (D, FF), D ** -0.5, 0.0625, ((0, 4), (1, 4)))
    up_weight = noise(arg_keys[2], (D, FF), D ** -0.5, 0.0625, ((0, 4), (1, 4)))
    down_weight = noise(arg_keys[3], (FF, D), FF ** -0.5, 0.046875, ((0, 4), (1, 4)))
    return dict(tokens=tokens, gate_weight=gate_weight, up_weight=up_weight, down_weight=down_weight)


def reference(tokens, gate_weight, up_weight, down_weight):
    block = D // N_WIDTH
    gate = jnp.zeros((TOKENS, FF), jnp.float32)
    up = jnp.zeros((TOKENS, FF), jnp.float32)
    for index in range(N_WIDTH):
        piece = tokens[:, index * block:(index + 1) * block]
        gate_part = jnp.dot(piece, gate_weight[index * block:(index + 1) * block], preferred_element_type=jnp.float32).astype(jnp.bfloat16)
        up_part = jnp.dot(piece, up_weight[index * block:(index + 1) * block], preferred_element_type=jnp.float32).astype(jnp.bfloat16)
        gate_part, up_part = lax.optimization_barrier((gate_part, up_part))
        gate = gate + gate_part.astype(jnp.float32)
        up = up + up_part.astype(jnp.float32)
    hidden = (jax.nn.silu(gate) * up).astype(jnp.bfloat16)
    output = jnp.dot(hidden, down_weight, preferred_element_type=jnp.float32)
    peak = jnp.max(jnp.abs(output), axis=0)
    scaled_output = (output / (peak + 1e-6)).astype(jnp.bfloat16)
    return scaled_output, peak / 448.0
```

```python
import jax
import jax.numpy as jnp
from jax import lax
from jax.experimental import pallas as pl
from jax.experimental.pallas import tpu as pltpu
from jax.sharding import PartitionSpec as P

CORES = 2
CHIPS = 2
WIDTH = CHIPS * CORES
RANKS = 4
AXIS = "tensor"


def swap(value, axis, mask):
    size = RANKS if axis == AXIS else WIDTH
    return lax.ppermute(value, axis, [(i, i ^ mask) for i in range(size)])


def widen(value):
    return value.astype(jnp.float32)


def narrow(value):
    return value.astype(jnp.bfloat16)


def dot(left, right):
    return jnp.dot(left, right, preferred_element_type=jnp.float32)


TILE = 512
GRANT = 4 << 20
COST = (1, 1)
PARTS = 3
VMEM = pl.BlockSpec(memory_space=pltpu.VMEM)


def project_kernel(block_ref, weight_ref, *refs):
    keep_ref, send_ref = refs[-2:]
    cut, units = keep_ref.shape[0], weight_ref.shape[1]
    first = 0 if len(refs) == 2 else units
    for start in range(0, units, TILE):
        value = narrow(dot(block_ref[...], weight_ref[:, start : start + TILE]))
        at = slice(first + start, first + start + TILE)
        keep_ref[:, at] = value[:cut]
        send_ref[:, at] = value[cut:]


def sums_kernel(keep_ref, *refs):
    cores, (mine_ref, send_ref) = refs[:-2], refs[-2:]
    cut = mine_ref.shape[0]
    at = 0
    for core_ref in cores:
        here = slice(at, at + core_ref.shape[1])
        at += core_ref.shape[1]
        chip = narrow(widen(keep_ref[:, here]) + widen(core_ref[...]))
        mine_ref[:, here] = chip[:cut]
        send_ref[:, here] = chip[cut:]


def hidden_kernel(mine_ref, got_ref, send_ref, share_ref, payload_ref, own_ref):
    units = own_ref.shape[1]
    for start in range(0, units, TILE):
        gate = slice(start, start + TILE)
        up = slice(units + start, units + start + TILE)
        both = [widen(mine_ref[:, at]) + widen(got_ref[:, at]) for at in (gate, up)]
        own_ref[:, gate] = narrow(jax.nn.silu(both[0]) * both[1])
    payload_ref[:, : 2 * units] = send_ref[...]
    payload_ref[:, 2 * units :] = own_ref[...]


def hidden_and_join_kernel(
    mine_ref, got_ref, send_ref, share_ref, payload_ref, own_ref, joined_ref
):
    units = own_ref.shape[1]
    cut = own_ref.shape[0]
    hidden_kernel(mine_ref, got_ref, send_ref, share_ref, payload_ref, own_ref)
    joined_ref[:cut] = share_ref[...]
    joined_ref[cut:] = got_ref[:, 2 * units :]


def last_hidden_kernel(mine_ref, got_ref, share_ref, own_ref, joined_ref):
    units = own_ref.shape[1]
    cut = own_ref.shape[0]
    for start in range(0, units, TILE):
        gate = slice(start, start + TILE)
        up = slice(units + start, units + start + TILE)
        both = [widen(mine_ref[:, at]) + widen(got_ref[:, at]) for at in (gate, up)]
        own_ref[:, gate] = narrow(jax.nn.silu(both[0]) * both[1])
    joined_ref[:cut] = share_ref[...]
    joined_ref[cut:] = got_ref[:, 2 * units :]


def output_kernel(mine_ref, core_ref, weight_ref, out_ref):
    hidden = jnp.concatenate([mine_ref[...], core_ref[...]])
    for start in range(0, weight_ref.shape[1], TILE):
        at = slice(start, start + TILE)
        out_ref[:, at] = dot(hidden, weight_ref[:, at]).astype(out_ref.dtype)


def call(kernel, shapes, args, cost, aliases, name):
    flops, size = cost
    return pl.pallas_call(
        kernel,
        out_shape=shapes,
        in_specs=[VMEM] * len(args),
        out_specs=jax.tree.map(lambda _: VMEM, shapes),
        input_output_aliases=aliases,
        compiler_params=pltpu.CompilerParams(vmem_limit_bytes=GRANT),
        cost_estimate=pl.CostEstimate(
            flops=flops, bytes_accessed=size, transcendentals=0
        ),
        name=name,
    )(*args)


def project(block, gate_weight, up_weight):
    rows, units = block.shape[0], gate_weight.shape[1]
    shape = jax.ShapeDtypeStruct((rows // 2, 2 * units), jnp.bfloat16)
    parts = call(
        project_kernel,
        (shape, shape),
        (block, gate_weight),
        COST,
        {},
        "gate",
    )
    return call(
        project_kernel,
        (shape, shape),
        (block, up_weight, *parts),
        COST,
        {2: 0, 3: 1},
        "up",
    )


def combine(mine, core, weight, dtype):
    rows = 2 * mine.shape[0]
    return call(
        output_kernel,
        jax.ShapeDtypeStruct((rows, weight.shape[1]), dtype),
        (mine, core, weight),
        COST,
        {},
        "down",
    )


def plain(tokens, gate_weight, up_weight, down_weight):
    units = gate_weight.shape[1]
    piece = lax.all_gather(tokens, AXIS, axis=0, tiled=True)
    parts = jnp.concatenate([dot(piece, gate_weight), dot(piece, up_weight)], axis=1)
    sums = widen(
        lax.psum_scatter(narrow(parts), "width", scatter_dimension=0, tiled=True)
    )
    share = narrow(jax.nn.silu(sums[:, :units]) * sums[:, units:])
    hidden = lax.all_gather(share, "width", axis=0, tiled=True)
    output = widen(
        lax.psum_scatter(
            narrow(dot(hidden, down_weight)), AXIS, scatter_dimension=0, tiled=True
        )
    )
    peak = lax.pmax(jnp.max(jnp.abs(output), axis=0), AXIS)
    return (narrow(output / (peak + 1e-06)), peak / 448.0)


def pipelined(tokens, gate_weight, up_weight, down_weight):
    units = gate_weight.shape[1]
    me = lax.axis_index("width")
    rows = tokens.shape[0] // WIDTH
    half = rows // 2
    clock = [None]

    def tick(*values):
        if clock[0] is not None:
            values = lax.optimization_barrier((*values, clock[0]))[:-1]
        return values if len(values) > 1 else values[0]

    def done(value):
        clock[0] = value
        return value

    def weave(*blocks):
        return jnp.concatenate(
            [
                block[p * n : (p + 1) * n]
                for p in range(WIDTH)
                for block, n in [(b, b.shape[0] // WIDTH) for b in blocks]
            ]
        )

    def begin(block):
        keep, send = project(tick(block), gate_weight, up_weight)
        done(keep)
        count = send.shape[1] // 128
        cuts = [count * i // PARTS * 128 for i in range(PARTS + 1)]
        return keep, [swap(send[:, a:b], "width", 1) for a, b in zip(cuts, cuts[1:])]

    def add_cores(keep, cores):
        keep, *cores = tick(keep, *cores)
        shape = jax.ShapeDtypeStruct((keep.shape[0] // 2, keep.shape[1]), keep.dtype)
        mine, send = call(
            sums_kernel, (shape, shape), (keep, *cores), COST, {}, "sums"
        )
        done(mine)
        return mine, send

    def hidden(mine, got, send=None, share=None):
        mine, got = tick(mine, got)
        own = jax.ShapeDtypeStruct((mine.shape[0], units), mine.dtype)
        joined = jax.ShapeDtypeStruct((2 * mine.shape[0], units), mine.dtype)
        payload = jax.ShapeDtypeStruct((mine.shape[0], 3 * units), mine.dtype)
        if send is None:
            own, joined = call(
                last_hidden_kernel,
                (own, joined),
                (mine, got, share),
                COST,
                {},
                "hidden",
            )
            payload = own
        elif share is None:
            payload, own = call(
                hidden_kernel, (payload, own), (mine, got, send, send), COST, {}, "hidden"
            )
            joined = None
        else:
            payload, own, joined = call(
                hidden_and_join_kernel,
                (payload, own, joined),
                (mine, got, send, share),
                COST,
                {},
                "hidden",
            )
        done(own)
        return swap(payload, "width", CORES), own, joined

    def finish(mine, core, dtype=jnp.bfloat16):
        mine, core = tick(mine, core)
        return done(combine(mine, core, down_weight, dtype))

    def split(value):
        n = value.shape[0] // (2 * WIDTH)
        parts = [value[i * n : (i + 1) * n] for i in range(2 * WIDTH)]
        return jnp.concatenate(parts[0::2]), jnp.concatenate(parts[1::2])

    order = [x * CORES + c for c in range(CORES) for x in range(CHIPS)]
    own = jnp.concatenate(
        [lax.dynamic_slice_in_dim(tokens, (me ^ j) * rows, rows, 0) for j in order]
    )
    (own,) = lax.optimization_barrier((own,))

    def halves(block):
        first = [block[p * rows : p * rows + half] for p in range(WIDTH)]
        second = [block[p * rows + half : (p + 1) * rows] for p in range(WIDTH)]
        return jnp.concatenate(first), jnp.concatenate(second)

    near = swap(own, AXIS, 1)
    cross = swap(own, AXIS, 2)

    mine0, send0 = add_cores(*begin(own))
    got0 = swap(send0, "width", CORES)
    near, cross = tick(near, cross)
    far = swap(cross, AXIS, 1)
    mine1, send1 = add_cores(*begin(near))

    got1, share0, _ = hidden(mine0, got0, send1)
    cross_first, cross_second = halves(cross)
    far = tick(far)
    far_first, far_second = halves(far)
    mine2, send2 = add_cores(*begin(weave(cross_first, far_first)))

    got2, share1, m0 = hidden(mine1, got1, send2, share0)
    b3 = begin(weave(cross_second, far_second))
    output = finish(m0, swap(m0, "width", 1), jnp.float32)
    mine3, send3 = add_cores(*b3)

    got3, share2, m1 = hidden(mine2, got2, send3, share1)
    p1 = swap(finish(m1, swap(m1, "width", 1)), AXIS, 1)

    got4, share3, m2 = hidden(mine3, got3, None, share2)
    p1 = tick(p1)
    output = done(output + widen(p1))
    cross2, far2 = split(finish(m2, swap(m2, "width", 1), jnp.float32))
    far2 = swap(narrow(far2), AXIS, 1)

    m3 = jnp.concatenate([share3, tick(got4)])
    cross3, far3 = split(finish(m3, swap(m3, "width", 1), jnp.float32))
    far3 = swap(narrow(far3), AXIS, 1)
    far2 = tick(far2)
    z2 = swap(done(narrow(cross2 + widen(far2))), AXIS, 2)
    far3 = tick(far3)
    z3 = swap(done(narrow(cross3 + widen(far3))), AXIS, 2)
    output = output + widen(weave(z2, z3))

    local_peak = jnp.max(jnp.abs(output), axis=0, keepdims=True)
    peak = local_peak
    for k in range(1, RANKS):
        peak = jnp.maximum(peak, swap(local_peak, AXIS, k))
    scaled = narrow(output / (peak + 1e-06))
    result = jnp.zeros_like(scaled)
    for place, j in enumerate(order):
        result = lax.dynamic_update_slice_in_dim(
            result, scaled[place * rows : (place + 1) * rows], (me ^ j) * rows, 0
        )
    return (result, peak[0] / 448.0)


def solution(mesh):
    in_specs = (
        P(("groups", "tensor"), "width"),
        P("width", "tensor"),
        P("width", "tensor"),
        P("tensor", "width"),
    )
    out_specs = (P(("groups", "tensor"), "width"), P(("groups", "width")))
    fits = mesh.shape[AXIS] == RANKS and mesh.shape["width"] == WIDTH
    return jax.shard_map(
        pipelined if fits else plain,
        mesh=mesh,
        in_specs=in_specs,
        out_specs=out_specs,
        check_vma=False,
    )
```

```python
import jax
import jax.numpy as jnp
from jax import lax
from jax.experimental import pallas as pl
from jax.experimental.pallas import tpu as pltpu
from jax.sharding import PartitionSpec as P

CORES = 2
CHIPS = 2
WIDTH = CHIPS * CORES
RANKS = 4
AXIS = "tensor"

TILE = 512
LANES = 128
GRANT = 4 << 20
VMEM = pl.BlockSpec(memory_space=pltpu.VMEM)
SMALL = (1, 1)


def swap(value, axis, mask):
    size = RANKS if axis == AXIS else WIDTH
    return lax.ppermute(value, axis, [(i, i ^ mask) for i in range(size)])


def swap_pieces(values):
    return [swap(value, "width", 1) for value in values]


def widen(value):
    return value.astype(jnp.float32)


def narrow(value):
    return value.astype(jnp.bfloat16)


def dot(left, right):
    return jnp.dot(left, right, preferred_element_type=jnp.float32)


def array(rows, columns, dtype=jnp.bfloat16):
    return jax.ShapeDtypeStruct((rows, columns), dtype)


def call(kernel, shapes, args, name, cost=SMALL, aliases=None):
    flops, size = cost
    return pl.pallas_call(
        kernel,
        out_shape=shapes,
        in_specs=[VMEM] * len(args),
        out_specs=jax.tree.map(lambda _: VMEM, shapes),
        input_output_aliases=aliases or {},
        compiler_params=pltpu.CompilerParams(vmem_limit_bytes=GRANT),
        cost_estimate=pl.CostEstimate(
            flops=flops, bytes_accessed=size, transcendentals=0
        ),
        name=name,
    )(*args)


def cuts(columns, count):
    return [columns // LANES * i // count * LANES for i in range(count + 1)]


def rows_of(order, index, rows):
    return [pl.multiple_of((index ^ j) * rows, rows) for j in order]


ORDER = [x * CORES + c for c in range(CORES) for x in range(CHIPS)]


def arrange_kernel(tokens_ref, own_ref):
    rows = tokens_ref.shape[0] // WIDTH
    half = rows // 2
    starts = rows_of(ORDER, lax.axis_index("width"), rows)
    at = 0
    for pair in (starts[:CHIPS], starts[CHIPS:]):
        for offset in (0, half):
            for start in pair:
                own_ref[at : at + half] = tokens_ref[
                    pl.ds(pl.multiple_of(start + offset, half), half)
                ]
                at += half


def halves_kernel(block_ref, first_ref, second_ref):
    n = block_ref.shape[0] // 4
    first_ref[:n] = block_ref[:n]
    second_ref[:n] = block_ref[n : 2 * n]
    first_ref[n:] = block_ref[2 * n : 3 * n]
    second_ref[n:] = block_ref[3 * n :]


def halves(block):
    shape = array(block.shape[0] // 2, block.shape[1])
    return call(halves_kernel, (shape, shape), (block,), "halves")


def project_kernel(plan, blocks, base, *refs):
    block_refs, weight_ref = refs[:blocks], refs[blocks]
    keep_ref, *send_refs = refs[len(refs) - 1 - sum(len(p[2]) - 1 for p in plan) :]
    parts = [ref[...] for ref in block_refs]
    if blocks > 1:
        n = parts[0].shape[0] // 2
        block = jnp.concatenate([p[:n] for p in parts] + [p[n:] for p in parts])
    else:
        block = parts[0]
    cut, units = keep_ref.shape[0], weight_ref.shape[1]
    edges = {0, units}
    edges.update(range(0, units, TILE))
    for _, _, bounds in plan:
        edges.update(b - base for b in bounds if base < b < base + units)
    edges = sorted(edges)
    for low, high in zip(edges, edges[1:]):
        value = narrow(dot(block, weight_ref[:, low:high]))
        keep_ref[:, base + low : base + high] = value[:cut]
        index = 0
        for first, count, bounds in plan:
            for a, b in zip(bounds, bounds[1:]):
                if a <= base + low < b:
                    rows = slice(cut + first, cut + first + count)
                    send_refs[index][:, base + low - a : base + high - a] = value[rows]
                index += 1


def project(blocks, weights, plan, cost=SMALL):
    rows, units = sum(b.shape[0] for b in blocks), weights[0].shape[1]
    shapes = [array(rows // 2, 2 * units)]
    for _, count, bounds in plan:
        shapes += [array(count, b - a) for a, b in zip(bounds, bounds[1:])]
    shapes = tuple(shapes)
    parts = ()
    for base, weight, name in zip((0, units), weights, ("gate", "up")):

        def kernel(*refs, base=base):
            project_kernel(plan, len(blocks), base, *refs)

        args = (*blocks, weight, *parts)
        aliases = {len(blocks) + 1 + i: i for i in range(len(parts))}
        parts = call(kernel, shapes, args, name, SMALL if base else cost, aliases)
    return parts


def sums_kernel(group, first, cores, keep_ref, *refs):
    cores, outs = refs[:cores], refs[cores:]
    rows, units = cores[0].shape[0], outs[0].shape[1]
    count, half = rows // group, group // 2
    each = 2 * count // len(outs)
    at = 0
    for core_ref in cores:
        low, high = at, at + core_ref.shape[1]
        at = high
        for a, b in ((low, min(high, units)), (max(low, units), high)):
            if a >= b:
                continue
            up = a >= units
            columns = slice(a - units, b - units) if up else slice(a, b)
            chip = narrow(
                widen(keep_ref[first : first + rows, a:b])
                + widen(core_ref[:, a - low : b - low])
            )
            base = each * half if up else 0
            for g in range(count):
                mine_ref, send_ref = outs[g // each * 2 : g // each * 2 + 2]
                to = slice(base + g % each * half, base + (g % each + 1) * half)
                mine_ref[to, columns] = chip[g * group : g * group + half]
                send_ref[to, columns] = chip[g * group + half : (g + 1) * group]


def add_cores(keep, cores, group, first=0, split=1):
    units = keep.shape[1] // 2
    shape = array(cores[0].shape[0] // split, units)

    def kernel(*refs):
        sums_kernel(group, first, len(cores), *refs)

    return call(kernel, (shape,) * (2 * split), (keep, *cores), "sums")


def activate(mine_ref, got_ref, own_ref):
    rows, units = own_ref.shape
    for start in range(0, units, TILE):
        at = slice(start, start + TILE)
        gate = widen(mine_ref[:rows, at]) + widen(got_ref[:rows, at])
        up = widen(mine_ref[rows:, at]) + widen(got_ref[rows : 2 * rows, at])
        own_ref[:, at] = narrow(jax.nn.silu(gate) * up)


def hidden(mine, got, send=None, share=None):
    rows, units = mine.shape[0] // 2, mine.shape[1]
    shapes = [array(rows, units)]
    args = [mine, got]
    if send is not None:
        shapes.append(array(send.shape[0] + rows, units))
        args.append(send)
    if share is not None:
        shapes.append(array(2 * share.shape[0], units))
        args.append(share)

    def kernel(*refs):
        refs = list(refs)
        mine_ref, got_ref = refs[:2]
        outs = refs[len(args) :]
        activate(mine_ref, got_ref, outs[0])
        if send is not None:
            outs[1][: send.shape[0]] = refs[2][...]
            outs[1][send.shape[0] :] = outs[0][...]
        if share is not None:
            n = share.shape[0]
            outs[-1][:n] = refs[len(args) - 1][...]
            outs[-1][n:] = got_ref[2 * rows : 2 * rows + n]

    return call(kernel, tuple(shapes), tuple(args), "hidden")


def join_kernel(share_ref, got_ref, out_ref):
    n = share_ref.shape[0]
    out_ref[:n] = share_ref[...]
    out_ref[n:] = got_ref[...]


def join(share, got):
    shape = array(2 * share.shape[0], share.shape[1])
    return call(join_kernel, shape, (share, got), "join")


def stack_kernel(first_ref, second_ref, out_ref):
    n = first_ref.shape[0]
    out_ref[:n] = first_ref[...]
    out_ref[n:] = second_ref[...]


def join_rows(first, second):
    shape = array(first.shape[0] + second.shape[0], first.shape[1])
    return call(stack_kernel, shape, (first, second), "stack")


def combine(mine, cores, weight, dtypes):
    rows, columns = 2 * mine.shape[0], weight.shape[1]
    count = len(dtypes)
    piece = rows // WIDTH // count
    shapes = tuple(array(rows // count, columns, dtype) for dtype in dtypes)

    def kernel(mine_ref, *refs):
        core_refs, weight_ref, outs = refs[: len(cores)], refs[len(cores)], refs[-count:]
        core = [ref[...] for ref in core_refs]
        core = jnp.concatenate(core, axis=1) if len(core) > 1 else core[0]
        value = jnp.concatenate([mine_ref[...], core])
        for start in range(0, columns, TILE):
            at = slice(start, start + TILE)
            result = dot(value, weight_ref[:, at])
            for p in range(WIDTH):
                for i, out_ref in enumerate(outs):
                    n = (p * count + i) * piece
                    out_ref[p * piece : (p + 1) * piece, at] = result[
                        n : n + piece
                    ].astype(out_ref.dtype)

    return call(kernel, shapes, (mine, *cores, weight), "down")


def add_kernel(part_ref, got_ref, out_ref):
    out_ref[...] = narrow(part_ref[...] + widen(got_ref[...]))


def scale_kernel(first_ref, second_ref, peak_ref, out_ref):
    rows = out_ref.shape[0] // WIDTH
    half = rows // 2
    starts = rows_of(ORDER, lax.axis_index("width"), rows)
    peak = peak_ref[...] + 1e-06
    for place, start in enumerate(starts):
        here = slice(place * half, (place + 1) * half)
        for offset, ref in ((0, first_ref), (half, second_ref)):
            to = pl.ds(pl.multiple_of(start + offset, half), half)
            out_ref[to] = narrow(ref[here] / peak)


def pipelined(tokens, gate_weight, up_weight, down_weight):
    units = gate_weight.shape[1]
    weights = (gate_weight, up_weight)
    rows = tokens.shape[0]
    stay = rows // 2
    group = stay // 2
    three, two = cuts(2 * units, 3), cuts(2 * units, 2)
    uneven = [0, three[2], 2 * units]
    clock = []

    def ticks(values):
        if clock:
            values = lax.optimization_barrier((*values, *clock))[: len(values)]
            clock[:] = [values[0]]
        return list(values)

    def tick(value):
        return ticks([value])[0]

    def done(values):
        clock.append(values[0] if isinstance(values, (tuple, list)) else values)
        return values

    def parts_of(mine, count):
        bounds = cuts(units, count)
        shapes = [array(mine.shape[0], b - a) for a, b in zip(bounds, bounds[1:])]

        def kernel(mine_ref, *outs):
            for a, b, out_ref in zip(bounds, bounds[1:], outs):
                out_ref[...] = mine_ref[:, a:b]

        return swap_pieces(call(kernel, tuple(shapes), (mine,), "pieces"))

    def arrange(block, cost=SMALL):
        return call(arrange_kernel, array(*block.shape), (block,), "arrange", cost)

    big, wide = rows * tokens.shape[1] * units, gate_weight.size
    near = swap(tokens, AXIS, 1)
    own = arrange(tokens, (8 * big, 4 * wide))
    own_first, own_second = halves(own)
    cross_first = swap(own_first, AXIS, 2)

    keep, *sends = project((own,), weights, [(0, stay, three)], (4 * big, 2 * wide))
    done(keep)
    cores = ticks(swap_pieces(sends))
    mine0, send0 = done(add_cores(keep, cores, group))
    got0 = swap(send0, "width", CORES)

    near = done(arrange(tick(near)))
    keep1, *sends = done(
        project((near,), weights, [(0, group, uneven), (group, group, two)])
    )
    cross_first, *sends = ticks([cross_first, *sends])
    sends5 = sends[2:]
    far_first = swap(cross_first, AXIS, 1)
    cross_second = swap(own_second, AXIS, 2)
    cores = ticks(swap_pieces(sends[:2]))
    mine1, send1 = done(add_cores(keep1, cores, group))

    got0 = tick(got0)
    share0, payload = done(hidden(mine0, got0, send1))
    got1 = swap(payload, "width", CORES)

    cores = ticks(swap_pieces(ticks(sends5)))
    mine5, send5 = done(add_cores(keep1, cores, group, group))

    got1 = tick(got1)
    share1, payload, joined0 = done(hidden(mine1, got1, send5, share0))
    got5 = swap(payload, "width", CORES)
    far_first = done(tick(far_first))
    keep, *sends = done(project((cross_first, far_first), weights, [(0, stay, three)]))
    cross_second, *sends = ticks([cross_second, *sends])
    far_second = swap(cross_second, AXIS, 1)
    cores = ticks(swap_pieces(sends))
    mine2, send2 = done(add_cores(keep, cores, group))

    got5 = tick(got5)
    share5, joined1 = done(hidden(mine5, got5, None, share1))
    got2 = swap(send2, "width", CORES)
    far_second = done(tick(far_second))
    keep, *sends = done(
        project((cross_second, far_second), weights, [(0, stay, three)])
    )
    got2, core1, *cores = ticks(
        [got2, swap(joined1, "width", 1), *swap_pieces(sends)]
    )

    (share2,) = done(hidden(mine2, got2))
    over2 = swap(share2, "width", CORES)
    mine3, send3, mine4, send4 = done(add_cores(keep, cores, group, split=2))
    payload = done(join_rows(send4, share5))
    (part1,) = done(combine(joined1, [core1], down_weight, (jnp.bfloat16,)))
    add1 = swap(part1, AXIS, 1)
    core0 = tick(swap(joined0, "width", 1))
    first, second = done(
        combine(joined0, [core0], down_weight, (jnp.float32, jnp.float32))
    )
    over2, payload = ticks([over2, payload])
    got4 = swap(payload, "width", CORES)
    joined2 = done(join(share2, over2))
    core2 = ticks(parts_of(joined2, 2))
    cross2, far2 = done(
        combine(joined2, core2, down_weight, (jnp.float32, jnp.bfloat16))
    )
    far2 = swap(far2, AXIS, 1)
    got3 = swap(tick(send3), "width", CORES)

    got4, add1 = ticks([got4, add1])
    share4, joined5 = done(hidden(mine4, got4, None, share5))
    over4 = swap(share4, "width", CORES)
    far2 = tick(far2)
    add2 = done(call(add_kernel, array(stay, tokens.shape[1]), (cross2, far2), "add"))
    add2 = swap(add2, AXIS, 2)
    over4 = tick(over4)
    joined4 = done(join(share4, over4))
    core4 = ticks(parts_of(joined4, 2))
    (far3,) = done(combine(joined4, core4, down_weight, (jnp.bfloat16,)))
    far3 = swap(far3, AXIS, 1)
    got3 = tick(got3)
    (share3,) = done(hidden(mine3, got3))
    over3 = swap(share3, "width", CORES)
    core5 = ticks(parts_of(joined5, 2))
    (part5,) = done(combine(joined5, core5, down_weight, (jnp.bfloat16,)))
    add5 = swap(part5, AXIS, 1)
    over3, add2 = ticks([over3, add2])
    joined3 = done(join(share3, over3))
    core3 = ticks(parts_of(joined3, 2))
    (cross3,) = done(combine(joined3, core3, down_weight, (jnp.float32,)))
    far3 = tick(far3)
    add3 = done(call(add_kernel, array(stay, tokens.shape[1]), (cross3, far3), "add"))
    add3 = swap(add3, AXIS, 2)

    first = first + widen(add1) + widen(add2)
    second = second + widen(add5) + widen(add3)
    local_peak = jnp.maximum(
        jnp.max(jnp.abs(first), axis=0, keepdims=True),
        jnp.max(jnp.abs(second), axis=0, keepdims=True),
    )
    peak = local_peak
    for k in range(1, RANKS):
        peak = jnp.maximum(peak, swap(local_peak, AXIS, k))
    scaled = call(scale_kernel, array(*tokens.shape), (first, second, peak), "scale")
    return (scaled, peak[0] / 448.0)


def plain(tokens, gate_weight, up_weight, down_weight):
    units = gate_weight.shape[1]
    piece = lax.all_gather(tokens, AXIS, axis=0, tiled=True)
    parts = jnp.concatenate([dot(piece, gate_weight), dot(piece, up_weight)], axis=1)
    sums = widen(
        lax.psum_scatter(narrow(parts), "width", scatter_dimension=0, tiled=True)
    )
    share = narrow(jax.nn.silu(sums[:, :units]) * sums[:, units:])
    hidden_units = lax.all_gather(share, "width", axis=0, tiled=True)
    output = widen(
        lax.psum_scatter(
            narrow(dot(hidden_units, down_weight)),
            AXIS,
            scatter_dimension=0,
            tiled=True,
        )
    )
    peak = lax.pmax(jnp.max(jnp.abs(output), axis=0), AXIS)
    return (narrow(output / (peak + 1e-06)), peak / 448.0)


def solution(mesh):
    in_specs = (
        P(("groups", "tensor"), "width"),
        P("width", "tensor"),
        P("width", "tensor"),
        P("tensor", "width"),
    )
    out_specs = (P(("groups", "tensor"), "width"), P(("groups", "width")))
    fits = mesh.shape[AXIS] == RANKS and mesh.shape["width"] == WIDTH
    return jax.shard_map(
        pipelined if fits else plain,
        mesh=mesh,
        in_specs=in_specs,
        out_specs=out_specs,
        check_vma=False,
    )
```

```python
import jax
import jax.numpy as jnp
from jax import lax
from jax.experimental import pallas as pl
from jax.experimental.pallas import tpu as pltpu
from jax.sharding import PartitionSpec as P

CORES = 2
CHIPS = 2
WIDTH = CHIPS * CORES
RANKS = 4
AXIS = "tensor"

TILE = 512
LANES = 128
GRANT = 4 << 20
VMEM = pl.BlockSpec(memory_space=pltpu.VMEM)
SMALL = (1, 1)


def swap(value, axis, mask):
    size = RANKS if axis == AXIS else WIDTH
    return lax.ppermute(value, axis, [(i, i ^ mask) for i in range(size)])


def swap_pieces(values):
    return [swap(value, "width", 1) for value in values]


def widen(value):
    return value.astype(jnp.float32)


def narrow(value):
    return value.astype(jnp.bfloat16)


def dot(left, right):
    return jnp.dot(left, right, preferred_element_type=jnp.float32)


def array(rows, columns, dtype=jnp.bfloat16):
    return jax.ShapeDtypeStruct((rows, columns), dtype)


def call(kernel, shapes, args, name, cost=SMALL, aliases=None):
    flops, size = cost
    return pl.pallas_call(
        kernel,
        out_shape=shapes,
        in_specs=[VMEM] * len(args),
        out_specs=jax.tree.map(lambda _: VMEM, shapes),
        input_output_aliases=aliases or {},
        compiler_params=pltpu.CompilerParams(vmem_limit_bytes=GRANT),
        cost_estimate=pl.CostEstimate(
            flops=flops, bytes_accessed=size, transcendentals=0
        ),
        name=name,
    )(*args)


def cuts(columns, count):
    return [columns // LANES * i // count * LANES for i in range(count + 1)]


def rows_of(order, index, rows):
    return [pl.multiple_of((index ^ j) * rows, rows) for j in order]


ORDER = [x * CORES + c for c in range(CORES) for x in range(CHIPS)]


def arrange_kernel(tokens_ref, own_ref):
    rows = tokens_ref.shape[0] // WIDTH
    half = rows // 2
    starts = rows_of(ORDER, lax.axis_index("width"), rows)
    at = 0
    for pair in (starts[:CHIPS], starts[CHIPS:]):
        for offset in (0, half):
            for start in pair:
                own_ref[at : at + half] = tokens_ref[
                    pl.ds(pl.multiple_of(start + offset, half), half)
                ]
                at += half


def halves_kernel(block_ref, first_ref, second_ref):
    n = block_ref.shape[0] // 4
    first_ref[:n] = block_ref[:n]
    second_ref[:n] = block_ref[n : 2 * n]
    first_ref[n:] = block_ref[2 * n : 3 * n]
    second_ref[n:] = block_ref[3 * n :]


def halves(block):
    shape = array(block.shape[0] // 2, block.shape[1])
    return call(halves_kernel, (shape, shape), (block,), "halves")


def project_kernel(plan, blocks, base, *refs):
    block_refs, weight_ref = refs[:blocks], refs[blocks]
    keep_ref, *send_refs = refs[len(refs) - 1 - sum(len(p[2]) - 1 for p in plan) :]
    parts = [ref[...] for ref in block_refs]
    if blocks > 1:
        n = parts[0].shape[0] // 2
        block = jnp.concatenate([p[:n] for p in parts] + [p[n:] for p in parts])
    else:
        block = parts[0]
    cut, units = keep_ref.shape[0], weight_ref.shape[1]
    edges = {0, units}
    edges.update(range(0, units, TILE))
    for _, _, bounds in plan:
        edges.update(b - base for b in bounds if base < b < base + units)
    edges = sorted(edges)
    for low, high in zip(edges, edges[1:]):
        value = narrow(dot(block, weight_ref[:, low:high]))
        keep_ref[:, base + low : base + high] = value[:cut]
        index = 0
        for first, count, bounds in plan:
            for a, b in zip(bounds, bounds[1:]):
                if a <= base + low < b:
                    rows = slice(cut + first, cut + first + count)
                    send_refs[index][:, base + low - a : base + high - a] = value[rows]
                index += 1


def project(blocks, weights, plan, cost=SMALL):
    rows, units = sum(b.shape[0] for b in blocks), weights[0].shape[1]
    shapes = [array(rows // 2, 2 * units)]
    for _, count, bounds in plan:
        shapes += [array(count, b - a) for a, b in zip(bounds, bounds[1:])]
    shapes = tuple(shapes)
    parts = ()
    for base, weight, name in zip((0, units), weights, ("gate", "up")):

        def kernel(*refs, base=base):
            project_kernel(plan, len(blocks), base, *refs)

        args = (*blocks, weight, *parts)
        aliases = {len(blocks) + 1 + i: i for i in range(len(parts))}
        parts = call(kernel, shapes, args, name, SMALL if base else cost, aliases)
    return parts


def sums_kernel(group, first, cores, keep_ref, *refs):
    cores, outs = refs[:cores], refs[cores:]
    rows, units = cores[0].shape[0], outs[0].shape[1]
    count, half = rows // group, group // 2
    each = 2 * count // len(outs)
    at = 0
    for core_ref in cores:
        low, high = at, at + core_ref.shape[1]
        at = high
        for a, b in ((low, min(high, units)), (max(low, units), high)):
            if a >= b:
                continue
            up = a >= units
            columns = slice(a - units, b - units) if up else slice(a, b)
            chip = narrow(
                widen(keep_ref[first : first + rows, a:b])
                + widen(core_ref[:, a - low : b - low])
            )
            base = each * half if up else 0
            for g in range(count):
                mine_ref, send_ref = outs[g // each * 2 : g // each * 2 + 2]
                to = slice(base + g % each * half, base + (g % each + 1) * half)
                mine_ref[to, columns] = chip[g * group : g * group + half]
                send_ref[to, columns] = chip[g * group + half : (g + 1) * group]


def add_cores(keep, cores, group, first=0, split=1):
    units = keep.shape[1] // 2
    shape = array(cores[0].shape[0] // split, units)

    def kernel(*refs):
        sums_kernel(group, first, len(cores), *refs)

    return call(kernel, (shape,) * (2 * split), (keep, *cores), "sums")


def activate(mine_ref, got_ref, own_ref):
    rows, units = own_ref.shape
    for start in range(0, units, TILE):
        at = slice(start, start + TILE)
        gate = widen(mine_ref[:rows, at]) + widen(got_ref[:rows, at])
        up = widen(mine_ref[rows:, at]) + widen(got_ref[rows : 2 * rows, at])
        own_ref[:, at] = narrow(jax.nn.silu(gate) * up)


def hidden(mine, got, send=None, share=None):
    rows, units = mine.shape[0] // 2, mine.shape[1]
    shapes = [array(rows, units)]
    args = [mine, got]
    if send is not None:
        shapes.append(array(send.shape[0] + rows, units))
        args.append(send)
    if share is not None:
        shapes.append(array(2 * share.shape[0], units))
        args.append(share)

    def kernel(*refs):
        refs = list(refs)
        mine_ref, got_ref = refs[:2]
        outs = refs[len(args) :]
        activate(mine_ref, got_ref, outs[0])
        if send is not None:
            outs[1][: send.shape[0]] = refs[2][...]
            outs[1][send.shape[0] :] = outs[0][...]
        if share is not None:
            n = share.shape[0]
            outs[-1][:n] = refs[len(args) - 1][...]
            outs[-1][n:] = got_ref[2 * rows : 2 * rows + n]

    return call(kernel, tuple(shapes), tuple(args), "hidden")


def join_kernel(share_ref, got_ref, out_ref):
    n = share_ref.shape[0]
    out_ref[:n] = share_ref[...]
    out_ref[n:] = got_ref[...]


def join(share, got):
    shape = array(2 * share.shape[0], share.shape[1])
    return call(join_kernel, shape, (share, got), "join")


def stack_kernel(first_ref, second_ref, out_ref):
    n = first_ref.shape[0]
    out_ref[:n] = first_ref[...]
    out_ref[n:] = second_ref[...]


def join_rows(first, second):
    shape = array(first.shape[0] + second.shape[0], first.shape[1])
    return call(stack_kernel, shape, (first, second), "stack")


def combine(mine, cores, weight, dtypes):
    rows, columns = 2 * mine.shape[0], weight.shape[1]
    count = len(dtypes)
    piece = rows // WIDTH // count
    shapes = tuple(array(rows // count, columns, dtype) for dtype in dtypes)

    def kernel(mine_ref, *refs):
        core_refs, weight_ref, outs = refs[: len(cores)], refs[len(cores)], refs[-count:]
        core = [ref[...] for ref in core_refs]
        core = jnp.concatenate(core, axis=1) if len(core) > 1 else core[0]
        value = jnp.concatenate([mine_ref[...], core])
        if rows < 128:
            value = jnp.concatenate([value] * (128 // rows))
        for start in range(0, columns, TILE):
            at = slice(start, start + TILE)
            result = dot(value, weight_ref[:, at])
            for p in range(WIDTH):
                for i, out_ref in enumerate(outs):
                    n = (p * count + i) * piece
                    out_ref[p * piece : (p + 1) * piece, at] = result[
                        n : n + piece
                    ].astype(out_ref.dtype)

    return call(kernel, shapes, (mine, *cores, weight), "down")


def add_kernel(part_ref, got_ref, out_ref):
    out_ref[...] = narrow(part_ref[...] + widen(got_ref[...]))


def scale_kernel(first_ref, second_ref, *refs):
    *peak_refs, out_ref, scales_ref = refs
    rows = out_ref.shape[0] // WIDTH
    half = rows // 2
    starts = rows_of(ORDER, lax.axis_index("width"), rows)
    peak = peak_refs[0][...]
    for peak_ref in peak_refs[1:]:
        peak = jnp.maximum(peak, peak_ref[...])
    scales_ref[...] = peak / 448.0
    peak = peak + 1e-06
    for place, start in enumerate(starts):
        here = slice(place * half, (place + 1) * half)
        for offset, ref in ((0, first_ref), (half, second_ref)):
            to = pl.ds(pl.multiple_of(start + offset, half), half)
            out_ref[to] = narrow(ref[here] / peak)


def pipelined(tokens, gate_weight, up_weight, down_weight):
    units = gate_weight.shape[1]
    weights = (gate_weight, up_weight)
    rows = tokens.shape[0]
    stay = rows // 2
    group = stay // 2
    three, two = cuts(2 * units, 3), cuts(2 * units, 2)
    uneven = [0, three[2], 2 * units]
    clock = []

    def ticks(values):
        if clock:
            values = lax.optimization_barrier((*values, *clock))[: len(values)]
            clock[:] = [values[0]]
        return list(values)

    def tick(value):
        return ticks([value])[0]

    def done(values):
        clock.append(values[0] if isinstance(values, (tuple, list)) else values)
        return values

    def parts_of(mine, count):
        bounds = cuts(units, count)
        shapes = [array(mine.shape[0], b - a) for a, b in zip(bounds, bounds[1:])]

        def kernel(mine_ref, *outs):
            for a, b, out_ref in zip(bounds, bounds[1:], outs):
                out_ref[...] = mine_ref[:, a:b]

        return swap_pieces(call(kernel, tuple(shapes), (mine,), "pieces"))

    def arrange(block, cost=SMALL):
        return call(arrange_kernel, array(*block.shape), (block,), "arrange", cost)

    big, wide = rows * tokens.shape[1] * units, gate_weight.size
    near = swap(tokens, AXIS, 1)
    own = arrange(tokens, (8 * big, 4 * wide))
    own_first, own_second = halves(own)
    cross_first = swap(own_first, AXIS, 2)

    keep, *sends = project((own,), weights, [(0, stay, three)], (4 * big, 2 * wide))
    done(keep)
    cores = ticks(swap_pieces(sends))
    mine0, send0 = done(add_cores(keep, cores, group))
    got0 = swap(send0, "width", CORES)

    near = done(arrange(tick(near)))
    keep1, *sends = done(
        project((near,), weights, [(0, group, uneven), (group, group, two)])
    )
    cross_first, *sends = ticks([cross_first, *sends])
    sends5 = sends[2:]
    far_first = swap(cross_first, AXIS, 1)
    cross_second = swap(own_second, AXIS, 2)
    cores = ticks(swap_pieces(sends[:2]))
    mine1, send1 = done(add_cores(keep1, cores, group))

    got0 = tick(got0)
    share0, payload = done(hidden(mine0, got0, send1))
    got1 = swap(payload, "width", CORES)

    cores = ticks(swap_pieces(ticks(sends5)))
    mine5, send5 = done(add_cores(keep1, cores, group, group))

    got1 = tick(got1)
    share1, payload, joined0 = done(hidden(mine1, got1, send5, share0))
    got5 = swap(payload, "width", CORES)
    far_first = done(tick(far_first))
    keep, *sends = done(project((cross_first, far_first), weights, [(0, stay, three)]))
    cross_second, *sends = ticks([cross_second, *sends])
    far_second = swap(cross_second, AXIS, 1)
    cores = ticks(swap_pieces(sends))
    mine2, send2 = done(add_cores(keep, cores, group))

    got5 = tick(got5)
    share5, joined1 = done(hidden(mine5, got5, None, share1))
    got2 = swap(send2, "width", CORES)
    core1 = ticks(parts_of(joined1, 2))
    (part1,) = done(combine(joined1, core1, down_weight, (jnp.bfloat16,)))
    add1 = swap(part1, AXIS, 1)
    far_second = done(tick(far_second))
    keep, *sends = done(
        project((cross_second, far_second), weights, [(0, stay, three)])
    )
    got2, *cores = ticks([got2, *swap_pieces(sends)])

    (share2,) = done(hidden(mine2, got2))
    over2 = swap(share2, "width", CORES)
    mine3, send3, mine4, send4 = done(add_cores(keep, cores, group, split=2))
    payload = done(join_rows(send4, share5))
    core0 = tick(swap(joined0, "width", 1))
    first, second = done(
        combine(joined0, [core0], down_weight, (jnp.float32, jnp.float32))
    )
    got4 = swap(payload, "width", CORES)
    over2, add1 = ticks([over2, add1])
    joined2 = done(join(share2, over2))
    core2 = ticks(parts_of(joined2, 2))
    cross2, far2 = done(
        combine(joined2, core2, down_weight, (jnp.float32, jnp.bfloat16))
    )
    far2 = swap(far2, AXIS, 1)
    got3 = swap(tick(send3), "width", CORES)

    got4 = tick(got4)
    share4, joined5 = done(hidden(mine4, got4, None, share5))
    over4 = swap(share4, "width", CORES)
    far2 = tick(far2)
    add2 = done(call(add_kernel, array(stay, tokens.shape[1]), (cross2, far2), "add"))
    add2 = swap(add2, AXIS, 2)
    over4 = tick(over4)
    joined4 = done(join(share4, over4))
    core4 = ticks(parts_of(joined4, 2))
    (far3,) = done(combine(joined4, core4, down_weight, (jnp.bfloat16,)))
    far3 = swap(far3, AXIS, 1)
    got3 = tick(got3)
    (share3,) = done(hidden(mine3, got3))
    over3 = swap(share3, "width", CORES)
    core5 = ticks(parts_of(joined5, 2))
    (part5,) = done(combine(joined5, core5, down_weight, (jnp.bfloat16,)))
    add5 = swap(part5, AXIS, 1)
    over3, add2 = ticks([over3, add2])
    joined3 = done(join(share3, over3))
    core3 = ticks(parts_of(joined3, 2))
    (cross3,) = done(combine(joined3, core3, down_weight, (jnp.float32,)))
    far3 = tick(far3)
    add3 = done(call(add_kernel, array(stay, tokens.shape[1]), (cross3, far3), "add"))
    add3 = swap(add3, AXIS, 2)

    first = first + widen(add1) + widen(add2)
    second = second + widen(add5) + widen(add3)
    local_peak = jnp.maximum(
        jnp.max(jnp.abs(first), axis=0, keepdims=True),
        jnp.max(jnp.abs(second), axis=0, keepdims=True),
    )
    peaks = [swap(local_peak, AXIS, k) for k in range(1, RANKS)]
    scaled, scales = call(
        scale_kernel,
        (array(*tokens.shape), array(1, tokens.shape[1], jnp.float32)),
        (first, second, local_peak, *peaks),
        "scale",
    )
    return (scaled, scales[0])


def plain(tokens, gate_weight, up_weight, down_weight):
    units = gate_weight.shape[1]
    piece = lax.all_gather(tokens, AXIS, axis=0, tiled=True)
    parts = jnp.concatenate([dot(piece, gate_weight), dot(piece, up_weight)], axis=1)
    sums = widen(
        lax.psum_scatter(narrow(parts), "width", scatter_dimension=0, tiled=True)
    )
    share = narrow(jax.nn.silu(sums[:, :units]) * sums[:, units:])
    hidden_units = lax.all_gather(share, "width", axis=0, tiled=True)
    output = widen(
        lax.psum_scatter(
            narrow(dot(hidden_units, down_weight)),
            AXIS,
            scatter_dimension=0,
            tiled=True,
        )
    )
    peak = lax.pmax(jnp.max(jnp.abs(output), axis=0), AXIS)
    return (narrow(output / (peak + 1e-06)), peak / 448.0)


def solution(mesh):
    in_specs = (
        P(("groups", "tensor"), "width"),
        P("width", "tensor"),
        P("width", "tensor"),
        P("tensor", "width"),
    )
    out_specs = (P(("groups", "tensor"), "width"), P(("groups", "width")))
    fits = mesh.shape[AXIS] == RANKS and mesh.shape["width"] == WIDTH
    return jax.shard_map(
        pipelined if fits else plain,
        mesh=mesh,
        in_specs=in_specs,
        out_specs=out_specs,
        check_vma=False,
    )
```

```python
import jax
import jax.numpy as jnp
from jax import lax
from jax.experimental import pallas as pl
from jax.experimental.pallas import tpu as pltpu
from jax.sharding import PartitionSpec as P

CORES = 2
CHIPS = 2
WIDTH = CHIPS * CORES
RANKS = 4
AXIS = "tensor"

TILE = 512
LANES = 128
GRANT = 4 << 20
VMEM = pl.BlockSpec(memory_space=pltpu.VMEM)
SMALL = (1, 1)


def swap(value, axis, mask):
    size = RANKS if axis == AXIS else WIDTH
    return lax.ppermute(value, axis, [(i, i ^ mask) for i in range(size)])


def swap_pieces(values):
    return [swap(value, "width", 1) for value in values]


def widen(value):
    return value.astype(jnp.float32)


def narrow(value):
    return value.astype(jnp.bfloat16)


def dot(left, right):
    return jnp.dot(left, right, preferred_element_type=jnp.float32)


def array(rows, columns, dtype=jnp.bfloat16):
    return jax.ShapeDtypeStruct((rows, columns), dtype)


def call(kernel, shapes, args, name, cost=SMALL, aliases=None):
    flops, size = cost
    return pl.pallas_call(
        kernel,
        out_shape=shapes,
        in_specs=[VMEM] * len(args),
        out_specs=jax.tree.map(lambda _: VMEM, shapes),
        input_output_aliases=aliases or {},
        compiler_params=pltpu.CompilerParams(vmem_limit_bytes=GRANT),
        cost_estimate=pl.CostEstimate(
            flops=flops, bytes_accessed=size, transcendentals=0
        ),
        name=name,
    )(*args)


def cuts(columns, count):
    return [columns // LANES * i // count * LANES for i in range(count + 1)]


def rows_of(order, index, rows):
    return [pl.multiple_of((index ^ j) * rows, rows) for j in order]


ORDER = [x * CORES + c for c in range(CORES) for x in range(CHIPS)]


def arrange_kernel(tokens_ref, own_ref):
    rows = tokens_ref.shape[0] // WIDTH
    half = rows // 2
    starts = rows_of(ORDER, lax.axis_index("width"), rows)
    at = 0
    for pair in (starts[:CHIPS], starts[CHIPS:]):
        for offset in (0, half):
            for start in pair:
                own_ref[at : at + half] = tokens_ref[
                    pl.ds(pl.multiple_of(start + offset, half), half)
                ]
                at += half


def halves_kernel(block_ref, first_ref, second_ref):
    n = block_ref.shape[0] // 4
    first_ref[:n] = block_ref[:n]
    second_ref[:n] = block_ref[n : 2 * n]
    first_ref[n:] = block_ref[2 * n : 3 * n]
    second_ref[n:] = block_ref[3 * n :]


def halves(block):
    shape = array(block.shape[0] // 2, block.shape[1])
    return call(halves_kernel, (shape, shape), (block,), "halves")


def project_kernel(plan, blocks, base, *refs):
    block_refs, weight_ref = refs[:blocks], refs[blocks]
    keep_ref, *send_refs = refs[len(refs) - 1 - sum(len(p[2]) - 1 for p in plan) :]
    parts = [ref[...] for ref in block_refs]
    if blocks > 1:
        n = parts[0].shape[0] // 2
        block = jnp.concatenate([p[:n] for p in parts] + [p[n:] for p in parts])
    else:
        block = parts[0]
    cut, units = keep_ref.shape[0], weight_ref.shape[1]
    edges = {0, units}
    edges.update(range(0, units, TILE))
    for _, _, bounds in plan:
        edges.update(b - base for b in bounds if base < b < base + units)
    edges = sorted(edges)
    for low, high in zip(edges, edges[1:]):
        value = narrow(dot(block, weight_ref[:, low:high]))
        keep_ref[:, base + low : base + high] = value[:cut]
        index = 0
        for first, count, bounds in plan:
            for a, b in zip(bounds, bounds[1:]):
                if a <= base + low < b:
                    rows = slice(cut + first, cut + first + count)
                    send_refs[index][:, base + low - a : base + high - a] = value[rows]
                index += 1


def project(blocks, weights, plan, cost=SMALL):
    rows, units = sum(b.shape[0] for b in blocks), weights[0].shape[1]
    shapes = [array(rows // 2, 2 * units)]
    for _, count, bounds in plan:
        shapes += [array(count, b - a) for a, b in zip(bounds, bounds[1:])]
    shapes = tuple(shapes)
    parts = ()
    for base, weight, name in zip((0, units), weights, ("gate", "up")):

        def kernel(*refs, base=base):
            project_kernel(plan, len(blocks), base, *refs)

        args = (*blocks, weight, *parts)
        aliases = {len(blocks) + 1 + i: i for i in range(len(parts))}
        parts = call(kernel, shapes, args, name, SMALL if base else cost, aliases)
    return parts


def sums_kernel(group, first, cores, keep_ref, *refs):
    cores, outs = refs[:cores], refs[cores:]
    rows, units = cores[0].shape[0], outs[0].shape[1]
    count, half = rows // group, group // 2
    each = 2 * count // len(outs)
    at = 0
    for core_ref in cores:
        low, high = at, at + core_ref.shape[1]
        at = high
        for a, b in ((low, min(high, units)), (max(low, units), high)):
            if a >= b:
                continue
            up = a >= units
            columns = slice(a - units, b - units) if up else slice(a, b)
            chip = narrow(
                widen(keep_ref[first : first + rows, a:b])
                + widen(core_ref[:, a - low : b - low])
            )
            base = each * half if up else 0
            for g in range(count):
                mine_ref, send_ref = outs[g // each * 2 : g // each * 2 + 2]
                to = slice(base + g % each * half, base + (g % each + 1) * half)
                mine_ref[to, columns] = chip[g * group : g * group + half]
                send_ref[to, columns] = chip[g * group + half : (g + 1) * group]


def add_cores(keep, cores, group, first=0, split=1):
    units = keep.shape[1] // 2
    shape = array(cores[0].shape[0] // split, units)

    def kernel(*refs):
        sums_kernel(group, first, len(cores), *refs)

    return call(kernel, (shape,) * (2 * split), (keep, *cores), "sums")


def activate(mine_ref, got_ref, own_ref):
    rows, units = own_ref.shape
    for start in range(0, units, TILE):
        at = slice(start, start + TILE)
        gate = widen(mine_ref[:rows, at]) + widen(got_ref[:rows, at])
        up = widen(mine_ref[rows:, at]) + widen(got_ref[rows : 2 * rows, at])
        own_ref[:, at] = narrow(jax.nn.silu(gate) * up)


def hidden(mine, got, send=None, share=None):
    rows, units = mine.shape[0] // 2, mine.shape[1]
    shapes = [array(rows, units)]
    args = [mine, got]
    if send is not None:
        shapes.append(array(send.shape[0] + rows, units))
        args.append(send)
    if share is not None:
        shapes.append(array(2 * share.shape[0], units))
        args.append(share)

    def kernel(*refs):
        refs = list(refs)
        mine_ref, got_ref = refs[:2]
        outs = refs[len(args) :]
        activate(mine_ref, got_ref, outs[0])
        if send is not None:
            outs[1][: send.shape[0]] = refs[2][...]
            outs[1][send.shape[0] :] = outs[0][...]
        if share is not None:
            n = share.shape[0]
            outs[-1][:n] = refs[len(args) - 1][...]
            outs[-1][n:] = got_ref[2 * rows : 2 * rows + n]

    return call(kernel, tuple(shapes), tuple(args), "hidden")


def join_kernel(share_ref, got_ref, out_ref):
    n = share_ref.shape[0]
    out_ref[:n] = share_ref[...]
    out_ref[n:] = got_ref[...]


def join(share, got):
    shape = array(2 * share.shape[0], share.shape[1])
    return call(join_kernel, shape, (share, got), "join")


def stack_kernel(first_ref, second_ref, out_ref):
    n = first_ref.shape[0]
    out_ref[:n] = first_ref[...]
    out_ref[n:] = second_ref[...]


def join_rows(first, second):
    shape = array(first.shape[0] + second.shape[0], first.shape[1])
    return call(stack_kernel, shape, (first, second), "stack")


def combine(mine, cores, weight, dtypes):
    rows, columns = 2 * mine.shape[0], weight.shape[1]
    count = len(dtypes)
    piece = rows // WIDTH // count
    shapes = tuple(array(rows // count, columns, dtype) for dtype in dtypes)

    def kernel(mine_ref, *refs):
        core_refs, weight_ref, outs = refs[: len(cores)], refs[len(cores)], refs[-count:]
        core = [ref[...] for ref in core_refs]
        core = jnp.concatenate(core, axis=1) if len(core) > 1 else core[0]
        value = jnp.concatenate([mine_ref[...], core])
        if rows < 128:
            value = jnp.concatenate([value] * (128 // rows))
        for start in range(0, columns, TILE):
            at = slice(start, start + TILE)
            result = dot(value, weight_ref[:, at])
            for p in range(WIDTH):
                for i, out_ref in enumerate(outs):
                    n = (p * count + i) * piece
                    out_ref[p * piece : (p + 1) * piece, at] = result[
                        n : n + piece
                    ].astype(out_ref.dtype)

    return call(kernel, shapes, (mine, *cores, weight), "down")


def add_kernel(part_ref, got_ref, out_ref):
    out_ref[...] = narrow(part_ref[...] + widen(got_ref[...]))


def scale_kernel(first_ref, second_ref, *refs):
    *peak_refs, out_ref, scales_ref = refs
    rows = out_ref.shape[0] // WIDTH
    half = rows // 2
    starts = rows_of(ORDER, lax.axis_index("width"), rows)
    peak = peak_refs[0][...]
    for peak_ref in peak_refs[1:]:
        peak = jnp.maximum(peak, peak_ref[...])
    scales_ref[...] = peak / 448.0
    peak = peak + 1e-06
    for place, start in enumerate(starts):
        here = slice(place * half, (place + 1) * half)
        for offset, ref in ((0, first_ref), (half, second_ref)):
            to = pl.ds(pl.multiple_of(start + offset, half), half)
            out_ref[to] = narrow(ref[here] / peak)


def pipelined(tokens, gate_weight, up_weight, down_weight):
    units = gate_weight.shape[1]
    weights = (gate_weight, up_weight)
    rows = tokens.shape[0]
    stay = rows // 2
    group = stay // 2
    three, two = cuts(2 * units, 3), cuts(2 * units, 2)
    uneven = [0, three[2], 2 * units]
    clock = []

    def ticks(values):
        if clock:
            values = lax.optimization_barrier((*values, *clock))[: len(values)]
            clock[:] = [values[0]]
        return list(values)

    def tick(value):
        return ticks([value])[0]

    def done(values):
        clock.append(values[0] if isinstance(values, (tuple, list)) else values)
        return values

    def parts_of(mine, count):
        bounds = cuts(units, count)
        shapes = [array(mine.shape[0], b - a) for a, b in zip(bounds, bounds[1:])]

        def kernel(mine_ref, *outs):
            for a, b, out_ref in zip(bounds, bounds[1:], outs):
                out_ref[...] = mine_ref[:, a:b]

        return swap_pieces(call(kernel, tuple(shapes), (mine,), "pieces"))

    def arrange(block, cost=SMALL):
        return call(arrange_kernel, array(*block.shape), (block,), "arrange", cost)

    big, wide = rows * tokens.shape[1] * units, gate_weight.size
    near = swap(tokens, AXIS, 1)
    own = arrange(tokens, (8 * big, 4 * wide))
    own_first, own_second = halves(own)
    cross_first = swap(own_first, AXIS, 2)

    keep, *sends = project((own,), weights, [(0, stay, three)], (4 * big, 2 * wide))
    done(keep)
    cores = ticks(swap_pieces(sends))
    mine0, send0 = done(add_cores(keep, cores, group))
    got0 = swap(send0, "width", CORES)

    near = done(arrange(tick(near)))
    keep1, *sends = done(
        project((near,), weights, [(0, group, uneven), (group, group, two)])
    )
    cross_first, *sends = ticks([cross_first, *sends])
    sends5 = sends[2:]
    far_first = swap(cross_first, AXIS, 1)
    cross_second = swap(own_second, AXIS, 2)
    cores = ticks(swap_pieces(sends[:2]))
    mine1, send1 = done(add_cores(keep1, cores, group))

    got0 = tick(got0)
    share0, payload = done(hidden(mine0, got0, send1))
    got1 = swap(payload, "width", CORES)

    cores = ticks(swap_pieces(ticks(sends5)))
    mine5, send5 = done(add_cores(keep1, cores, group, group))

    got1 = tick(got1)
    share1, payload, joined0 = done(hidden(mine1, got1, send5, share0))
    got5 = swap(payload, "width", CORES)
    far_first = done(tick(far_first))
    keep, *sends = done(project((cross_first, far_first), weights, [(0, stay, three)]))
    cross_second, *sends = ticks([cross_second, *sends])
    far_second = swap(cross_second, AXIS, 1)
    cores = ticks(swap_pieces(sends))
    mine2, send2 = done(add_cores(keep, cores, group))

    got5 = tick(got5)
    share5, joined1 = done(hidden(mine5, got5, None, share1))
    got2 = swap(send2, "width", CORES)
    core1 = ticks(parts_of(joined1, 2))
    (part1,) = done(combine(joined1, core1, down_weight, (jnp.bfloat16,)))
    add1 = swap(part1, AXIS, 1)
    far_second = done(tick(far_second))
    keep, *sends = done(
        project((cross_second, far_second), weights, [(0, stay, three)])
    )
    got2, *cores = ticks([got2, *swap_pieces(sends)])

    (share2,) = done(hidden(mine2, got2))
    over2 = swap(share2, "width", CORES)
    mine3, send3, mine4, send4 = done(add_cores(keep, cores, group, split=2))
    payload = done(join_rows(send4, share5))
    core0 = tick(swap(joined0, "width", 1))
    first, second = done(
        combine(joined0, [core0], down_weight, (jnp.float32, jnp.float32))
    )
    got4 = swap(payload, "width", CORES)
    over2, add1 = ticks([over2, add1])
    joined2 = done(join(share2, over2))
    core2 = ticks(parts_of(joined2, 2))
    cross2, far2 = done(
        combine(joined2, core2, down_weight, (jnp.float32, jnp.bfloat16))
    )
    far2 = swap(far2, AXIS, 1)
    got3 = swap(tick(send3), "width", CORES)

    got4 = tick(got4)
    share4, joined5 = done(hidden(mine4, got4, None, share5))
    over4 = swap(share4, "width", CORES)
    far2 = tick(far2)
    add2 = done(call(add_kernel, array(stay, tokens.shape[1]), (cross2, far2), "add"))
    add2 = swap(add2, AXIS, 2)
    over4 = tick(over4)
    joined4 = done(join(share4, over4))
    core4 = ticks(parts_of(joined4, 2))
    (far3,) = done(combine(joined4, core4, down_weight, (jnp.bfloat16,)))
    far3 = swap(far3, AXIS, 1)
    got3 = tick(got3)
    (share3,) = done(hidden(mine3, got3))
    over3 = swap(share3, "width", CORES)
    core5 = ticks(parts_of(joined5, 2))
    (part5,) = done(combine(joined5, core5, down_weight, (jnp.bfloat16,)))
    add5 = swap(part5, AXIS, 1)
    over3, add2 = ticks([over3, add2])
    joined3 = done(join(share3, over3))
    core3 = ticks(parts_of(joined3, 2))
    (cross3,) = done(combine(joined3, core3, down_weight, (jnp.float32,)))
    far3 = tick(far3)
    add3 = done(call(add_kernel, array(stay, tokens.shape[1]), (cross3, far3), "add"))
    add3 = swap(add3, AXIS, 2)

    first = first + widen(add1) + widen(add2)
    second = second + widen(add5) + widen(add3)
    local_peak = jnp.maximum(
        jnp.max(jnp.abs(first), axis=0, keepdims=True),
        jnp.max(jnp.abs(second), axis=0, keepdims=True),
    )
    peaks = [swap(local_peak, AXIS, k) for k in range(RANKS - 1, 0, -1)]
    scaled, scales = call(
        scale_kernel,
        (array(*tokens.shape), array(1, tokens.shape[1], jnp.float32)),
        (first, second, local_peak, *peaks),
        "scale",
    )
    return (scaled, scales[0])


def plain(tokens, gate_weight, up_weight, down_weight):
    units = gate_weight.shape[1]
    piece = lax.all_gather(tokens, AXIS, axis=0, tiled=True)
    parts = jnp.concatenate([dot(piece, gate_weight), dot(piece, up_weight)], axis=1)
    sums = widen(
        lax.psum_scatter(narrow(parts), "width", scatter_dimension=0, tiled=True)
    )
    share = narrow(jax.nn.silu(sums[:, :units]) * sums[:, units:])
    hidden_units = lax.all_gather(share, "width", axis=0, tiled=True)
    output = widen(
        lax.psum_scatter(
            narrow(dot(hidden_units, down_weight)),
            AXIS,
            scatter_dimension=0,
            tiled=True,
        )
    )
    peak = lax.pmax(jnp.max(jnp.abs(output), axis=0), AXIS)
    return (narrow(output / (peak + 1e-06)), peak / 448.0)


def solution(mesh):
    in_specs = (
        P(("groups", "tensor"), "width"),
        P("width", "tensor"),
        P("width", "tensor"),
        P("tensor", "width"),
    )
    out_specs = (P(("groups", "tensor"), "width"), P(("groups", "width")))
    fits = mesh.shape[AXIS] == RANKS and mesh.shape["width"] == WIDTH
    return jax.shard_map(
        pipelined if fits else plain,
        mesh=mesh,
        in_specs=in_specs,
        out_specs=out_specs,
        check_vma=False,
    )
```

```python
import jax
import jax.numpy as jnp
from jax import lax
from jax.experimental import pallas as pl
from jax.experimental.pallas import tpu as pltpu
from jax.sharding import PartitionSpec as P

CORES = 2
CHIPS = 2
WIDTH = CHIPS * CORES
RANKS = 4
AXIS = "tensor"

TILE = 512
LANES = 128
GRANT = 4 << 20
VMEM = pl.BlockSpec(memory_space=pltpu.VMEM)
SMALL = (1, 1)


def swap(value, axis, mask):
    size = RANKS if axis == AXIS else WIDTH
    return lax.ppermute(value, axis, [(i, i ^ mask) for i in range(size)])


def swap_pieces(values):
    return [swap(value, "width", 1) for value in values]


def widen(value):
    return value.astype(jnp.float32)


def narrow(value):
    return value.astype(jnp.bfloat16)


def dot(left, right):
    return jnp.dot(left, right, preferred_element_type=jnp.float32)


def array(rows, columns, dtype=jnp.bfloat16):
    return jax.ShapeDtypeStruct((rows, columns), dtype)


def call(kernel, shapes, args, name, cost=SMALL, aliases=None):
    flops, size = cost
    return pl.pallas_call(
        kernel,
        out_shape=shapes,
        in_specs=[VMEM] * len(args),
        out_specs=jax.tree.map(lambda _: VMEM, shapes),
        input_output_aliases=aliases or {},
        compiler_params=pltpu.CompilerParams(vmem_limit_bytes=GRANT),
        cost_estimate=pl.CostEstimate(
            flops=flops, bytes_accessed=size, transcendentals=0
        ),
        name=name,
    )(*args)


def cuts(columns, count):
    return [columns // LANES * i // count * LANES for i in range(count + 1)]


def rows_of(order, index, rows):
    return [pl.multiple_of((index ^ j) * rows, rows) for j in order]


ORDER = [x * CORES + c for c in range(CORES) for x in range(CHIPS)]


def arrange_kernel(tokens_ref, own_ref):
    rows = tokens_ref.shape[0] // WIDTH
    half = rows // 2
    starts = rows_of(ORDER, lax.axis_index("width"), rows)
    at = 0
    for pair in (starts[:CHIPS], starts[CHIPS:]):
        for offset in (0, half):
            for start in pair:
                own_ref[at : at + half] = tokens_ref[
                    pl.ds(pl.multiple_of(start + offset, half), half)
                ]
                at += half


def halves_kernel(block_ref, first_ref, second_ref):
    n = block_ref.shape[0] // 4
    first_ref[:n] = block_ref[:n]
    second_ref[:n] = block_ref[n : 2 * n]
    first_ref[n:] = block_ref[2 * n : 3 * n]
    second_ref[n:] = block_ref[3 * n :]


def halves(block):
    shape = array(block.shape[0] // 2, block.shape[1])
    return call(halves_kernel, (shape, shape), (block,), "halves")


def project_kernel(plan, blocks, base, *refs):
    block_refs, weight_ref = refs[:blocks], refs[blocks]
    keep_ref, *send_refs = refs[len(refs) - 1 - sum(len(p[2]) - 1 for p in plan) :]
    parts = [ref[...] for ref in block_refs]
    if blocks > 1:
        n = parts[0].shape[0] // 2
        block = jnp.concatenate([p[:n] for p in parts] + [p[n:] for p in parts])
    else:
        block = parts[0]
    cut, units = keep_ref.shape[0], weight_ref.shape[1]
    edges = {0, units}
    edges.update(range(0, units, TILE))
    for _, _, bounds in plan:
        edges.update(b - base for b in bounds if base < b < base + units)
    edges = sorted(edges)
    for low, high in zip(edges, edges[1:]):
        value = narrow(dot(block, weight_ref[:, low:high]))
        keep_ref[:, base + low : base + high] = value[:cut]
        index = 0
        for first, count, bounds in plan:
            for a, b in zip(bounds, bounds[1:]):
                if a <= base + low < b:
                    rows = slice(cut + first, cut + first + count)
                    send_refs[index][:, base + low - a : base + high - a] = value[rows]
                index += 1


def project(blocks, weights, plan, cost=SMALL):
    rows, units = sum(b.shape[0] for b in blocks), weights[0].shape[1]
    shapes = [array(rows // 2, 2 * units)]
    for _, count, bounds in plan:
        shapes += [array(count, b - a) for a, b in zip(bounds, bounds[1:])]
    shapes = tuple(shapes)
    parts = ()
    for base, weight, name in zip((0, units), weights, ("gate", "up")):

        def kernel(*refs, base=base):
            project_kernel(plan, len(blocks), base, *refs)

        args = (*blocks, weight, *parts)
        aliases = {len(blocks) + 1 + i: i for i in range(len(parts))}
        parts = call(kernel, shapes, args, name, SMALL if base else cost, aliases)
    return parts


def sums_kernel(group, first, cores, keep_ref, *refs):
    cores, outs = refs[:cores], refs[cores:]
    rows, units = cores[0].shape[0], outs[0].shape[1]
    count, half = rows // group, group // 2
    each = 2 * count // len(outs)
    at = 0
    for core_ref in cores:
        low, high = at, at + core_ref.shape[1]
        at = high
        for a, b in ((low, min(high, units)), (max(low, units), high)):
            if a >= b:
                continue
            up = a >= units
            columns = slice(a - units, b - units) if up else slice(a, b)
            chip = narrow(
                widen(keep_ref[first : first + rows, a:b])
                + widen(core_ref[:, a - low : b - low])
            )
            base = each * half if up else 0
            for g in range(count):
                mine_ref, send_ref = outs[g // each * 2 : g // each * 2 + 2]
                to = slice(base + g % each * half, base + (g % each + 1) * half)
                mine_ref[to, columns] = chip[g * group : g * group + half]
                send_ref[to, columns] = chip[g * group + half : (g + 1) * group]


def add_cores(keep, cores, group, first=0, split=1):
    units = keep.shape[1] // 2
    shape = array(cores[0].shape[0] // split, units)

    def kernel(*refs):
        sums_kernel(group, first, len(cores), *refs)

    return call(kernel, (shape,) * (2 * split), (keep, *cores), "sums")


def activate(mine_ref, got_ref, own_ref):
    rows, units = own_ref.shape
    for start in range(0, units, TILE):
        at = slice(start, start + TILE)
        gate = widen(mine_ref[:rows, at]) + widen(got_ref[:rows, at])
        up = widen(mine_ref[rows:, at]) + widen(got_ref[rows : 2 * rows, at])
        own_ref[:, at] = narrow(jax.nn.silu(gate) * up)


def hidden(mine, got, send=None, share=None):
    rows, units = mine.shape[0] // 2, mine.shape[1]
    shapes = [array(rows, units)]
    args = [mine, got]
    if send is not None:
        shapes.append(array(send.shape[0] + rows, units))
        args.append(send)
    if share is not None:
        shapes.append(array(2 * share.shape[0], units))
        args.append(share)

    def kernel(*refs):
        refs = list(refs)
        mine_ref, got_ref = refs[:2]
        outs = refs[len(args) :]
        activate(mine_ref, got_ref, outs[0])
        if send is not None:
            outs[1][: send.shape[0]] = refs[2][...]
            outs[1][send.shape[0] :] = outs[0][...]
        if share is not None:
            n = share.shape[0]
            outs[-1][:n] = refs[len(args) - 1][...]
            outs[-1][n:] = got_ref[2 * rows : 2 * rows + n]

    return call(kernel, tuple(shapes), tuple(args), "hidden")


def join_kernel(share_ref, got_ref, out_ref):
    n = share_ref.shape[0]
    out_ref[:n] = share_ref[...]
    out_ref[n:] = got_ref[...]


def join(share, got):
    shape = array(2 * share.shape[0], share.shape[1])
    return call(join_kernel, shape, (share, got), "join")


def stack_kernel(first_ref, second_ref, out_ref):
    n = first_ref.shape[0]
    out_ref[:n] = first_ref[...]
    out_ref[n:] = second_ref[...]


def join_rows(first, second):
    shape = array(first.shape[0] + second.shape[0], first.shape[1])
    return call(stack_kernel, shape, (first, second), "stack")


def combine(mine, cores, weight, dtypes):
    rows, columns = 2 * mine.shape[0], weight.shape[1]
    count = len(dtypes)
    piece = rows // WIDTH // count
    shapes = tuple(array(rows // count, columns, dtype) for dtype in dtypes)

    def kernel(mine_ref, *refs):
        core_refs, weight_ref, outs = refs[: len(cores)], refs[len(cores)], refs[-count:]
        core = [ref[...] for ref in core_refs]
        core = jnp.concatenate(core, axis=1) if len(core) > 1 else core[0]
        value = jnp.concatenate([mine_ref[...], core])
        if rows < 128:
            value = jnp.concatenate([value] * (128 // rows))
        for start in range(0, columns, TILE):
            at = slice(start, start + TILE)
            result = dot(value, weight_ref[:, at])
            for p in range(WIDTH):
                for i, out_ref in enumerate(outs):
                    n = (p * count + i) * piece
                    out_ref[p * piece : (p + 1) * piece, at] = result[
                        n : n + piece
                    ].astype(out_ref.dtype)

    return call(kernel, shapes, (mine, *cores, weight), "down")


def add_kernel(part_ref, got_ref, out_ref):
    out_ref[...] = narrow(part_ref[...] + widen(got_ref[...]))


def peak_kernel(one_ref, other_ref, out_ref):
    out_ref[...] = jnp.maximum(one_ref[...], other_ref[...])


def scale_kernel(first_ref, second_ref, *refs):
    *peak_refs, out_ref, scales_ref = refs
    rows = out_ref.shape[0] // WIDTH
    half = rows // 2
    starts = rows_of(ORDER, lax.axis_index("width"), rows)
    peak = peak_refs[0][...]
    for peak_ref in peak_refs[1:]:
        peak = jnp.maximum(peak, peak_ref[...])
    scales_ref[...] = peak / 448.0
    peak = peak + 1e-06
    for place, start in enumerate(starts):
        here = slice(place * half, (place + 1) * half)
        for offset, ref in ((0, first_ref), (half, second_ref)):
            to = pl.ds(pl.multiple_of(start + offset, half), half)
            out_ref[to] = narrow(ref[here] / peak)


def pipelined(tokens, gate_weight, up_weight, down_weight):
    units = gate_weight.shape[1]
    weights = (gate_weight, up_weight)
    rows = tokens.shape[0]
    stay = rows // 2
    group = stay // 2
    three, two = cuts(2 * units, 3), cuts(2 * units, 2)
    uneven = [0, three[2], 2 * units]
    clock = []

    def ticks(values):
        if clock:
            values = lax.optimization_barrier((*values, *clock))[: len(values)]
            clock[:] = [values[0]]
        return list(values)

    def tick(value):
        return ticks([value])[0]

    def done(values):
        clock.append(values[0] if isinstance(values, (tuple, list)) else values)
        return values

    def parts_of(mine, count):
        bounds = cuts(units, count)
        shapes = [array(mine.shape[0], b - a) for a, b in zip(bounds, bounds[1:])]

        def kernel(mine_ref, *outs):
            for a, b, out_ref in zip(bounds, bounds[1:], outs):
                out_ref[...] = mine_ref[:, a:b]

        return swap_pieces(call(kernel, tuple(shapes), (mine,), "pieces"))

    def arrange(block, cost=SMALL):
        return call(arrange_kernel, array(*block.shape), (block,), "arrange", cost)

    big, wide = rows * tokens.shape[1] * units, gate_weight.size
    near = swap(tokens, AXIS, 1)
    own = arrange(tokens, (8 * big, 4 * wide))
    own_first, own_second = halves(own)
    cross_first = swap(own_first, AXIS, 2)

    keep, *sends = project((own,), weights, [(0, stay, three)], (4 * big, 2 * wide))
    done(keep)
    cores = ticks(swap_pieces(sends))
    mine0, send0 = done(add_cores(keep, cores, group))
    got0 = swap(send0, "width", CORES)

    near = done(arrange(tick(near)))
    keep1, *sends = done(
        project((near,), weights, [(0, group, uneven), (group, group, two)])
    )
    cross_first, *sends = ticks([cross_first, *sends])
    sends5 = sends[2:]
    far_first = swap(cross_first, AXIS, 1)
    cross_second = swap(own_second, AXIS, 2)
    cores = ticks(swap_pieces(sends[:2]))
    mine1, send1 = done(add_cores(keep1, cores, group))

    got0 = tick(got0)
    share0, payload = done(hidden(mine0, got0, send1))
    got1 = swap(payload, "width", CORES)

    cores = ticks(swap_pieces(ticks(sends5)))
    mine5, send5 = done(add_cores(keep1, cores, group, group))

    got1 = tick(got1)
    share1, payload, joined0 = done(hidden(mine1, got1, send5, share0))
    got5 = swap(payload, "width", CORES)
    far_first = done(tick(far_first))
    keep, *sends = done(project((cross_first, far_first), weights, [(0, stay, three)]))
    cross_second, *sends = ticks([cross_second, *sends])
    far_second = swap(cross_second, AXIS, 1)
    cores = ticks(swap_pieces(sends))
    mine2, send2 = done(add_cores(keep, cores, group))

    got5 = tick(got5)
    share5, joined1 = done(hidden(mine5, got5, None, share1))
    got2 = swap(send2, "width", CORES)
    core1 = ticks(parts_of(joined1, 2))
    (part1,) = done(combine(joined1, core1, down_weight, (jnp.bfloat16,)))
    add1 = swap(part1, AXIS, 1)
    far_second = done(tick(far_second))
    keep, *sends = done(
        project((cross_second, far_second), weights, [(0, stay, three)])
    )
    got2, *cores = ticks([got2, *swap_pieces(sends)])

    (share2,) = done(hidden(mine2, got2))
    over2 = swap(share2, "width", CORES)
    mine3, send3, mine4, send4 = done(add_cores(keep, cores, group, split=2))
    payload = done(join_rows(send4, share5))
    core0 = tick(swap(joined0, "width", 1))
    first, second = done(
        combine(joined0, [core0], down_weight, (jnp.float32, jnp.float32))
    )
    got4 = swap(tick(payload), "width", CORES)
    over2, add1 = ticks([over2, add1])
    joined2 = done(join(share2, over2))
    core2 = ticks(parts_of(joined2, 3))
    cross2, far2 = done(
        combine(joined2, core2, down_weight, (jnp.float32, jnp.bfloat16))
    )
    far2 = swap(far2, AXIS, 1)

    got4 = tick(got4)
    share4, joined5 = done(hidden(mine4, got4, None, share5))
    over4 = swap(share4, "width", CORES)
    over4 = tick(over4)
    joined4 = done(join(share4, over4))
    got3 = swap(tick(send3), "width", CORES)
    core4 = ticks(parts_of(joined4, 2))
    (far3,) = done(combine(joined4, core4, down_weight, (jnp.bfloat16,)))
    far3 = swap(far3, AXIS, 1)
    far2 = tick(far2)
    add2 = done(call(add_kernel, array(stay, tokens.shape[1]), (cross2, far2), "add"))
    add2 = swap(add2, AXIS, 2)
    got3 = tick(got3)
    (share3,) = done(hidden(mine3, got3))
    over3 = swap(share3, "width", CORES)
    core5 = ticks(parts_of(joined5, 2))
    (part5,) = done(combine(joined5, core5, down_weight, (jnp.bfloat16,)))
    add5 = swap(part5, AXIS, 1)
    over3 = tick(over3)
    joined3 = done(join(share3, over3))
    core3 = ticks(parts_of(joined3, 2))
    (cross3,) = done(combine(joined3, core3, down_weight, (jnp.float32,)))
    far3, add2 = ticks([far3, add2])
    add3 = done(call(add_kernel, array(stay, tokens.shape[1]), (cross3, far3), "add"))
    add3 = swap(add3, AXIS, 2)

    first = first + widen(add1) + widen(add2)
    second = second + widen(add5) + widen(add3)
    local_peak = jnp.maximum(
        jnp.max(jnp.abs(first), axis=0, keepdims=True),
        jnp.max(jnp.abs(second), axis=0, keepdims=True),
    )
    pair_peak = call(
        peak_kernel, array(*local_peak.shape, jnp.float32), (local_peak, swap(local_peak, AXIS, 2)), "peak"
    )
    peaks = [swap(pair_peak, AXIS, 1)]
    scaled, scales = call(
        scale_kernel,
        (array(*tokens.shape), array(1, tokens.shape[1], jnp.float32)),
        (first, second, pair_peak, *peaks),
        "scale",
    )
    return (scaled, scales[0])


def plain(tokens, gate_weight, up_weight, down_weight):
    units = gate_weight.shape[1]
    piece = lax.all_gather(tokens, AXIS, axis=0, tiled=True)
    parts = jnp.concatenate([dot(piece, gate_weight), dot(piece, up_weight)], axis=1)
    sums = widen(
        lax.psum_scatter(narrow(parts), "width", scatter_dimension=0, tiled=True)
    )
    share = narrow(jax.nn.silu(sums[:, :units]) * sums[:, units:])
    hidden_units = lax.all_gather(share, "width", axis=0, tiled=True)
    output = widen(
        lax.psum_scatter(
            narrow(dot(hidden_units, down_weight)),
            AXIS,
            scatter_dimension=0,
            tiled=True,
        )
    )
    peak = lax.pmax(jnp.max(jnp.abs(output), axis=0), AXIS)
    return (narrow(output / (peak + 1e-06)), peak / 448.0)


def solution(mesh):
    in_specs = (
        P(("groups", "tensor"), "width"),
        P("width", "tensor"),
        P("width", "tensor"),
        P("tensor", "width"),
    )
    out_specs = (P(("groups", "tensor"), "width"), P(("groups", "width")))
    fits = mesh.shape[AXIS] == RANKS and mesh.shape["width"] == WIDTH
    return jax.shard_map(
        pipelined if fits else plain,
        mesh=mesh,
        in_specs=in_specs,
        out_specs=out_specs,
        check_vma=False,
    )
```

```python
import jax
import jax.numpy as jnp
from jax import lax
from jax.experimental import pallas as pl
from jax.experimental.pallas import tpu as pltpu
from jax.sharding import PartitionSpec as P

CORES = 2
CHIPS = 2
WIDTH = CHIPS * CORES
RANKS = 4
AXIS = "tensor"

TILE = 512
LANES = 128
GRANT = 4 << 20
VMEM = pl.BlockSpec(memory_space=pltpu.VMEM)
SMALL = (1, 1)


def swap(value, axis, mask):
    size = RANKS if axis == AXIS else WIDTH
    return lax.ppermute(value, axis, [(i, i ^ mask) for i in range(size)])


def swap_pieces(values):
    return [swap(value, "width", 1) for value in values]


def widen(value):
    return value.astype(jnp.float32)


def narrow(value):
    return value.astype(jnp.bfloat16)


def dot(left, right):
    return jnp.dot(left, right, preferred_element_type=jnp.float32)


def array(rows, columns, dtype=jnp.bfloat16):
    return jax.ShapeDtypeStruct((rows, columns), dtype)


def call(kernel, shapes, args, name, cost=SMALL, aliases=None):
    flops, size = cost
    return pl.pallas_call(
        kernel,
        out_shape=shapes,
        in_specs=[VMEM] * len(args),
        out_specs=jax.tree.map(lambda _: VMEM, shapes),
        input_output_aliases=aliases or {},
        compiler_params=pltpu.CompilerParams(vmem_limit_bytes=GRANT),
        cost_estimate=pl.CostEstimate(
            flops=flops, bytes_accessed=size, transcendentals=0
        ),
        name=name,
    )(*args)


def cuts(columns, count):
    return [columns // LANES * i // count * LANES for i in range(count + 1)]


def rows_of(order, index, rows):
    return [pl.multiple_of((index ^ j) * rows, rows) for j in order]


ORDER = [x * CORES + c for c in range(CORES) for x in range(CHIPS)]


def arrange_kernel(tokens_ref, own_ref):
    rows = tokens_ref.shape[0] // WIDTH
    half = rows // 2
    starts = rows_of(ORDER, lax.axis_index("width"), rows)
    at = 0
    for pair in (starts[:CHIPS], starts[CHIPS:]):
        for offset in (0, half):
            for start in pair:
                own_ref[at : at + half] = tokens_ref[
                    pl.ds(pl.multiple_of(start + offset, half), half)
                ]
                at += half


def halves_kernel(block_ref, first_ref, second_ref):
    n = block_ref.shape[0] // 4
    first_ref[:n] = block_ref[:n]
    second_ref[:n] = block_ref[n : 2 * n]
    first_ref[n:] = block_ref[2 * n : 3 * n]
    second_ref[n:] = block_ref[3 * n :]


def halves(block):
    shape = array(block.shape[0] // 2, block.shape[1])
    return call(halves_kernel, (shape, shape), (block,), "halves")


def project_kernel(plan, blocks, base, *refs):
    block_refs, weight_ref = refs[:blocks], refs[blocks]
    keep_ref, *send_refs = refs[len(refs) - 1 - sum(len(p[2]) - 1 for p in plan) :]
    parts = [ref[...] for ref in block_refs]
    if blocks > 1:
        n = parts[0].shape[0] // 2
        block = jnp.concatenate([p[:n] for p in parts] + [p[n:] for p in parts])
    else:
        block = parts[0]
    cut, units = keep_ref.shape[0], weight_ref.shape[1]
    edges = {0, units}
    edges.update(range(0, units, TILE))
    for _, _, bounds in plan:
        edges.update(b - base for b in bounds if base < b < base + units)
    edges = sorted(edges)
    for low, high in zip(edges, edges[1:]):
        value = narrow(dot(block, weight_ref[:, low:high]))
        keep_ref[:, base + low : base + high] = value[:cut]
        index = 0
        for first, count, bounds in plan:
            for a, b in zip(bounds, bounds[1:]):
                if a <= base + low < b:
                    rows = slice(cut + first, cut + first + count)
                    send_refs[index][:, base + low - a : base + high - a] = value[rows]
                index += 1


def project(blocks, weights, plan, cost=SMALL):
    rows, units = sum(b.shape[0] for b in blocks), weights[0].shape[1]
    shapes = [array(rows // 2, 2 * units)]
    for _, count, bounds in plan:
        shapes += [array(count, b - a) for a, b in zip(bounds, bounds[1:])]
    shapes = tuple(shapes)
    parts = ()
    for base, weight, name in zip((0, units), weights, ("gate", "up")):

        def kernel(*refs, base=base):
            project_kernel(plan, len(blocks), base, *refs)

        args = (*blocks, weight, *parts)
        aliases = {len(blocks) + 1 + i: i for i in range(len(parts))}
        parts = call(kernel, shapes, args, name, SMALL if base else cost, aliases)
    return parts


def sums_kernel(group, first, cores, keep_ref, *refs):
    cores, outs = refs[:cores], refs[cores:]
    rows, units = cores[0].shape[0], outs[0].shape[1]
    count, half = rows // group, group // 2
    each = 2 * count // len(outs)
    at = 0
    for core_ref in cores:
        low, high = at, at + core_ref.shape[1]
        at = high
        for a, b in ((low, min(high, units)), (max(low, units), high)):
            if a >= b:
                continue
            up = a >= units
            columns = slice(a - units, b - units) if up else slice(a, b)
            chip = narrow(
                widen(keep_ref[first : first + rows, a:b])
                + widen(core_ref[:, a - low : b - low])
            )
            base = each * half if up else 0
            for g in range(count):
                mine_ref, send_ref = outs[g // each * 2 : g // each * 2 + 2]
                to = slice(base + g % each * half, base + (g % each + 1) * half)
                mine_ref[to, columns] = chip[g * group : g * group + half]
                send_ref[to, columns] = chip[g * group + half : (g + 1) * group]


def add_cores(keep, cores, group, first=0, split=1):
    units = keep.shape[1] // 2
    shape = array(cores[0].shape[0] // split, units)

    def kernel(*refs):
        sums_kernel(group, first, len(cores), *refs)

    return call(kernel, (shape,) * (2 * split), (keep, *cores), "sums")


def activate(mine_ref, got_ref, own_ref):
    rows, units = own_ref.shape
    for start in range(0, units, TILE):
        at = slice(start, start + TILE)
        gate = widen(mine_ref[:rows, at]) + widen(got_ref[:rows, at])
        up = widen(mine_ref[rows:, at]) + widen(got_ref[rows : 2 * rows, at])
        own_ref[:, at] = narrow(jax.nn.silu(gate) * up)


def hidden(mine, got, send=None, share=None):
    rows, units = mine.shape[0] // 2, mine.shape[1]
    shapes = [array(rows, units)]
    args = [mine, got]
    if send is not None:
        shapes.append(array(send.shape[0] + rows, units))
        args.append(send)
    if share is not None:
        shapes.append(array(2 * share.shape[0], units))
        args.append(share)

    def kernel(*refs):
        refs = list(refs)
        mine_ref, got_ref = refs[:2]
        outs = refs[len(args) :]
        activate(mine_ref, got_ref, outs[0])
        if send is not None:
            outs[1][: send.shape[0]] = refs[2][...]
            outs[1][send.shape[0] :] = outs[0][...]
        if share is not None:
            n = share.shape[0]
            outs[-1][:n] = refs[len(args) - 1][...]
            outs[-1][n:] = got_ref[2 * rows : 2 * rows + n]

    return call(kernel, tuple(shapes), tuple(args), "hidden")


def join_kernel(share_ref, got_ref, out_ref):
    n = share_ref.shape[0]
    out_ref[:n] = share_ref[...]
    out_ref[n:] = got_ref[...]


def join(share, got):
    shape = array(2 * share.shape[0], share.shape[1])
    return call(join_kernel, shape, (share, got), "join")


def stack_kernel(first_ref, second_ref, out_ref):
    n = first_ref.shape[0]
    out_ref[:n] = first_ref[...]
    out_ref[n:] = second_ref[...]


def join_rows(first, second):
    shape = array(first.shape[0] + second.shape[0], first.shape[1])
    return call(stack_kernel, shape, (first, second), "stack")


def combine(mine, cores, weight, dtypes):
    rows, columns = 2 * mine.shape[0], weight.shape[1]
    count = len(dtypes)
    piece = rows // WIDTH // count
    shapes = tuple(array(rows // count, columns, dtype) for dtype in dtypes)

    def kernel(mine_ref, *refs):
        core_refs, weight_ref, outs = refs[: len(cores)], refs[len(cores)], refs[-count:]
        core = [ref[...] for ref in core_refs]
        core = jnp.concatenate(core, axis=1) if len(core) > 1 else core[0]
        value = jnp.concatenate([mine_ref[...], core])
        if rows < 128:
            value = jnp.concatenate([value] * (128 // rows))
        for start in range(0, columns, TILE):
            at = slice(start, start + TILE)
            result = dot(value, weight_ref[:, at])
            for p in range(WIDTH):
                for i, out_ref in enumerate(outs):
                    n = (p * count + i) * piece
                    out_ref[p * piece : (p + 1) * piece, at] = result[
                        n : n + piece
                    ].astype(out_ref.dtype)

    return call(kernel, shapes, (mine, *cores, weight), "down")


def join_columns(first, second):
    cut = first.shape[1]

    def kernel(first_ref, second_ref, out_ref):
        out_ref[:, :cut] = first_ref[...]
        out_ref[:, cut:] = second_ref[...]

    shape = array(first.shape[0], cut + second.shape[1])
    return call(kernel, shape, (first, second), "columns")


def combine_parts(mine, cores, weight, dtypes):
    args = (*mine, *cores)
    rows, columns = sum(v.shape[0] for v in args), weight.shape[1]
    count = len(dtypes)
    piece = rows // WIDTH // count
    shapes = tuple(array(rows // count, columns, dtype) for dtype in dtypes)

    def kernel(*refs):
        outs, weight_ref = refs[-count:], refs[len(args)]
        value = jnp.concatenate([ref[...] for ref in refs[: len(args)]])
        if rows < 128:
            value = jnp.concatenate([value] * (128 // rows))
        for start in range(0, columns, TILE):
            at = slice(start, start + TILE)
            result = dot(value, weight_ref[:, at])
            for p in range(WIDTH):
                for i, out_ref in enumerate(outs):
                    n = (p * count + i) * piece
                    out_ref[p * piece : (p + 1) * piece, at] = result[
                        n : n + piece
                    ].astype(out_ref.dtype)

    return call(kernel, shapes, (*args, weight), "down")


def add_kernel(part_ref, got_ref, out_ref):
    out_ref[...] = narrow(part_ref[...] + widen(got_ref[...]))


def peak_kernel(one_ref, other_ref, out_ref):
    out_ref[...] = jnp.maximum(one_ref[...], other_ref[...])


def scale_kernel(first_ref, second_ref, *refs):
    *peak_refs, out_ref, scales_ref = refs
    rows = out_ref.shape[0] // WIDTH
    half = rows // 2
    starts = rows_of(ORDER, lax.axis_index("width"), rows)
    peak = peak_refs[0][...]
    for peak_ref in peak_refs[1:]:
        peak = jnp.maximum(peak, peak_ref[...])
    scales_ref[...] = peak / 448.0
    peak = peak + 1e-06
    for place, start in enumerate(starts):
        here = slice(place * half, (place + 1) * half)
        for offset, ref in ((0, first_ref), (half, second_ref)):
            to = pl.ds(pl.multiple_of(start + offset, half), half)
            out_ref[to] = narrow(ref[here] / peak)


def pipelined(tokens, gate_weight, up_weight, down_weight):
    units = gate_weight.shape[1]
    weights = (gate_weight, up_weight)
    rows = tokens.shape[0]
    stay = rows // 2
    group = stay // 2
    three, two = cuts(2 * units, 3), cuts(2 * units, 2)
    uneven = [0, three[2], 2 * units]
    clock = []

    def ticks(values):
        if clock:
            values = lax.optimization_barrier((*values, *clock))[: len(values)]
            clock[:] = [values[0]]
        return list(values)

    def tick(value):
        return ticks([value])[0]

    def done(values):
        clock.append(values[0] if isinstance(values, (tuple, list)) else values)
        return values

    def parts_of(mine, count):
        bounds = cuts(units, count)
        shapes = [array(mine.shape[0], b - a) for a, b in zip(bounds, bounds[1:])]

        def kernel(mine_ref, *outs):
            for a, b, out_ref in zip(bounds, bounds[1:], outs):
                out_ref[...] = mine_ref[:, a:b]

        return swap_pieces(call(kernel, tuple(shapes), (mine,), "pieces"))

    def arrange(block, cost=SMALL):
        return call(arrange_kernel, array(*block.shape), (block,), "arrange", cost)

    big, wide = rows * tokens.shape[1] * units, gate_weight.size
    near = swap(tokens, AXIS, 1)
    own = arrange(tokens, (8 * big, 4 * wide))
    own_first, own_second = halves(own)
    cross_first = swap(own_first, AXIS, 2)

    keep, *sends = project((own,), weights, [(0, stay, three)], (4 * big, 2 * wide))
    done(keep)
    cores = ticks(swap_pieces(sends))
    mine0, send0 = done(add_cores(keep, cores, group))
    got0 = swap(send0, "width", CORES)

    near = done(arrange(tick(near)))
    keep1, *sends = done(
        project((near,), weights, [(0, group, uneven), (group, group, two)])
    )
    cross_first, *sends = ticks([cross_first, *sends])
    sends5 = sends[2:]
    far_first = swap(cross_first, AXIS, 1)
    cross_second = swap(own_second, AXIS, 2)
    cores = ticks(swap_pieces(sends[:2]))
    mine1, send1 = done(add_cores(keep1, cores, group))

    got0 = tick(got0)
    share0, payload = done(hidden(mine0, got0, send1))
    got1 = swap(payload, "width", CORES)

    cores = ticks(swap_pieces(ticks(sends5)))
    mine5, send5 = done(add_cores(keep1, cores, group, group))

    got1 = tick(got1)
    share1, payload, joined0 = done(hidden(mine1, got1, send5, share0))
    got5 = swap(payload, "width", CORES)
    far_first = done(tick(far_first))
    keep, *sends = done(project((cross_first, far_first), weights, [(0, stay, three)]))
    cross_second, *sends = ticks([cross_second, *sends])
    far_second = swap(cross_second, AXIS, 1)
    cores = ticks(swap_pieces(sends))
    mine2, send2 = done(add_cores(keep, cores, group))

    got5 = tick(got5)
    share5, joined1 = done(hidden(mine5, got5, None, share1))
    got2 = swap(send2, "width", CORES)
    core1 = ticks(parts_of(joined1, 2))
    (part1,) = done(combine(joined1, core1, down_weight, (jnp.bfloat16,)))
    add1 = swap(part1, AXIS, 1)
    far_second = done(tick(far_second))
    keep, *sends = done(
        project((cross_second, far_second), weights, [(0, stay, three)])
    )
    got2, *cores = ticks([got2, *swap_pieces(sends)])

    (share2,) = done(hidden(mine2, got2))
    over2 = swap(share2, "width", CORES)
    early2 = swap(share2, "width", 1)
    mine3, send3, mine4, send4 = done(add_cores(keep, cores, group, split=2))
    payload = done(join_rows(send4, share5))
    core0 = tick(swap(joined0, "width", 1))
    first, second = done(
        combine(joined0, [core0], down_weight, (jnp.float32, jnp.float32))
    )
    got4 = swap(tick(payload), "width", CORES)
    over2, add1, early2 = ticks([over2, add1, early2])
    done(over2)
    core2 = ticks(parts_of(over2, 2))
    cross2, far2 = done(
        combine_parts(
            (share2, over2),
            (early2, done(join_columns(*core2))),
            down_weight,
            (jnp.float32, jnp.bfloat16),
        )
    )
    far2 = swap(far2, AXIS, 1)

    got4 = tick(got4)
    share4, joined5 = done(hidden(mine4, got4, None, share5))
    over4 = swap(share4, "width", CORES)
    early4 = swap(share4, "width", 1)
    over4, early4 = ticks([over4, early4])
    done(over4)
    got3 = swap(tick(send3), "width", CORES)
    core4 = tick(swap(over4, "width", 1))
    (far3,) = done(
        combine_parts((share4, over4), (early4, core4), down_weight, (jnp.bfloat16,))
    )
    far3 = swap(far3, AXIS, 1)
    far2 = tick(far2)
    add2 = done(call(add_kernel, array(stay, tokens.shape[1]), (cross2, far2), "add"))
    add2 = swap(add2, AXIS, 2)
    got3 = tick(got3)
    (share3,) = done(hidden(mine3, got3))
    over3 = swap(share3, "width", CORES)
    core5 = ticks(parts_of(joined5, 2))
    (part5,) = done(combine(joined5, core5, down_weight, (jnp.bfloat16,)))
    add5 = swap(part5, AXIS, 1)
    over3 = tick(over3)
    joined3 = done(join(share3, over3))
    core3 = ticks(parts_of(joined3, 2))
    (cross3,) = done(combine(joined3, core3, down_weight, (jnp.float32,)))
    far3, add2 = ticks([far3, add2])
    add3 = done(call(add_kernel, array(stay, tokens.shape[1]), (cross3, far3), "add"))
    add3 = swap(add3, AXIS, 2)

    first = first + widen(add1) + widen(add2)
    second = second + widen(add5) + widen(add3)
    local_peak = jnp.maximum(
        jnp.max(jnp.abs(first), axis=0, keepdims=True),
        jnp.max(jnp.abs(second), axis=0, keepdims=True),
    )
    pair_peak = call(
        peak_kernel, array(*local_peak.shape, jnp.float32), (local_peak, swap(local_peak, AXIS, 2)), "peak"
    )
    peaks = [swap(pair_peak, AXIS, 1)]
    scaled, scales = call(
        scale_kernel,
        (array(*tokens.shape), array(1, tokens.shape[1], jnp.float32)),
        (first, second, pair_peak, *peaks),
        "scale",
    )
    return (scaled, scales[0])


def plain(tokens, gate_weight, up_weight, down_weight):
    units = gate_weight.shape[1]
    piece = lax.all_gather(tokens, AXIS, axis=0, tiled=True)
    parts = jnp.concatenate([dot(piece, gate_weight), dot(piece, up_weight)], axis=1)
    sums = widen(
        lax.psum_scatter(narrow(parts), "width", scatter_dimension=0, tiled=True)
    )
    share = narrow(jax.nn.silu(sums[:, :units]) * sums[:, units:])
    hidden_units = lax.all_gather(share, "width", axis=0, tiled=True)
    output = widen(
        lax.psum_scatter(
            narrow(dot(hidden_units, down_weight)),
            AXIS,
            scatter_dimension=0,
            tiled=True,
        )
    )
    peak = lax.pmax(jnp.max(jnp.abs(output), axis=0), AXIS)
    return (narrow(output / (peak + 1e-06)), peak / 448.0)


def solution(mesh):
    in_specs = (
        P(("groups", "tensor"), "width"),
        P("width", "tensor"),
        P("width", "tensor"),
        P("tensor", "width"),
    )
    out_specs = (P(("groups", "tensor"), "width"), P(("groups", "width")))
    fits = mesh.shape[AXIS] == RANKS and mesh.shape["width"] == WIDTH
    return jax.shard_map(
        pipelined if fits else plain,
        mesh=mesh,
        in_specs=in_specs,
        out_specs=out_specs,
        check_vma=False,
    )
```

```python
import jax
import jax.numpy as jnp
from jax import lax
from jax.experimental import pallas as pl
from jax.experimental.pallas import tpu as pltpu
from jax.sharding import PartitionSpec as P

CORES = 2
CHIPS = 2
WIDTH = CHIPS * CORES
RANKS = 4
AXIS = "tensor"

TILE = 512
LANES = 128
GRANT = 4 << 20
VMEM = pl.BlockSpec(memory_space=pltpu.VMEM)
SMALL = (1, 1)


def swap(value, axis, mask):
    size = RANKS if axis == AXIS else WIDTH
    return lax.ppermute(value, axis, [(i, i ^ mask) for i in range(size)])


def swap_pieces(values):
    return [swap(value, "width", 1) for value in values]


def widen(value):
    return value.astype(jnp.float32)


def narrow(value):
    return value.astype(jnp.bfloat16)


def dot(left, right):
    return jnp.dot(left, right, preferred_element_type=jnp.float32)


def array(rows, columns, dtype=jnp.bfloat16):
    return jax.ShapeDtypeStruct((rows, columns), dtype)


def call(kernel, shapes, args, name, cost=SMALL, aliases=None):
    flops, size = cost
    return pl.pallas_call(
        kernel,
        out_shape=shapes,
        in_specs=[VMEM] * len(args),
        out_specs=jax.tree.map(lambda _: VMEM, shapes),
        input_output_aliases=aliases or {},
        compiler_params=pltpu.CompilerParams(vmem_limit_bytes=GRANT),
        cost_estimate=pl.CostEstimate(
            flops=flops, bytes_accessed=size, transcendentals=0
        ),
        name=name,
    )(*args)


def cuts(columns, count):
    return [columns // LANES * i // count * LANES for i in range(count + 1)]


def rows_of(order, index, rows):
    return [pl.multiple_of((index ^ j) * rows, rows) for j in order]


ORDER = [x * CORES + c for c in range(CORES) for x in range(CHIPS)]


def arrange_kernel(tokens_ref, own_ref):
    rows = tokens_ref.shape[0] // WIDTH
    half = rows // 2
    starts = rows_of(ORDER, lax.axis_index("width"), rows)
    at = 0
    for pair in (starts[:CHIPS], starts[CHIPS:]):
        for offset in (0, half):
            for start in pair:
                own_ref[at : at + half] = tokens_ref[
                    pl.ds(pl.multiple_of(start + offset, half), half)
                ]
                at += half


def halves_kernel(block_ref, first_ref, second_ref):
    n = block_ref.shape[0] // 4
    first_ref[:n] = block_ref[:n]
    second_ref[:n] = block_ref[n : 2 * n]
    first_ref[n:] = block_ref[2 * n : 3 * n]
    second_ref[n:] = block_ref[3 * n :]


def halves(block):
    shape = array(block.shape[0] // 2, block.shape[1])
    return call(halves_kernel, (shape, shape), (block,), "halves")


def project_kernel(plan, blocks, base, *refs):
    block_refs, weight_ref = refs[:blocks], refs[blocks]
    keep_ref, *send_refs = refs[len(refs) - 1 - sum(len(p[2]) - 1 for p in plan) :]
    parts = [ref[...] for ref in block_refs]
    if blocks > 1:
        n = parts[0].shape[0] // 2
        block = jnp.concatenate([p[:n] for p in parts] + [p[n:] for p in parts])
    else:
        block = parts[0]
    cut, units = keep_ref.shape[0], weight_ref.shape[1]
    edges = {0, units}
    edges.update(range(0, units, TILE))
    for _, _, bounds in plan:
        edges.update(b - base for b in bounds if base < b < base + units)
    edges = sorted(edges)
    for low, high in zip(edges, edges[1:]):
        value = narrow(dot(block, weight_ref[:, low:high]))
        keep_ref[:, base + low : base + high] = value[:cut]
        index = 0
        for first, count, bounds in plan:
            for a, b in zip(bounds, bounds[1:]):
                if a <= base + low < b:
                    rows = slice(cut + first, cut + first + count)
                    send_refs[index][:, base + low - a : base + high - a] = value[rows]
                index += 1


def project(blocks, weights, plan, cost=SMALL):
    rows, units = sum(b.shape[0] for b in blocks), weights[0].shape[1]
    shapes = [array(rows // 2, 2 * units)]
    for _, count, bounds in plan:
        shapes += [array(count, b - a) for a, b in zip(bounds, bounds[1:])]
    shapes = tuple(shapes)
    parts = ()
    for base, weight, name in zip((0, units), weights, ("gate", "up")):

        def kernel(*refs, base=base):
            project_kernel(plan, len(blocks), base, *refs)

        args = (*blocks, weight, *parts)
        aliases = {len(blocks) + 1 + i: i for i in range(len(parts))}
        parts = call(kernel, shapes, args, name, SMALL if base else cost, aliases)
    return parts


def sums_kernel(group, first, cores, keep_ref, *refs):
    cores, outs = refs[:cores], refs[cores:]
    rows, units = cores[0].shape[0], outs[0].shape[1]
    count, half = rows // group, group // 2
    each = 2 * count // len(outs)
    at = 0
    for core_ref in cores:
        low, high = at, at + core_ref.shape[1]
        at = high
        for a, b in ((low, min(high, units)), (max(low, units), high)):
            if a >= b:
                continue
            up = a >= units
            columns = slice(a - units, b - units) if up else slice(a, b)
            chip = narrow(
                widen(keep_ref[first : first + rows, a:b])
                + widen(core_ref[:, a - low : b - low])
            )
            base = each * half if up else 0
            for g in range(count):
                mine_ref, send_ref = outs[g // each * 2 : g // each * 2 + 2]
                to = slice(base + g % each * half, base + (g % each + 1) * half)
                mine_ref[to, columns] = chip[g * group : g * group + half]
                send_ref[to, columns] = chip[g * group + half : (g + 1) * group]


def add_cores(keep, cores, group, first=0, split=1):
    units = keep.shape[1] // 2
    shape = array(cores[0].shape[0] // split, units)

    def kernel(*refs):
        sums_kernel(group, first, len(cores), *refs)

    return call(kernel, (shape,) * (2 * split), (keep, *cores), "sums")


def activate(mine_ref, got_ref, own_ref):
    rows, units = own_ref.shape
    for start in range(0, units, TILE):
        at = slice(start, start + TILE)
        gate = widen(mine_ref[:rows, at]) + widen(got_ref[:rows, at])
        up = widen(mine_ref[rows:, at]) + widen(got_ref[rows : 2 * rows, at])
        own_ref[:, at] = narrow(jax.nn.silu(gate) * up)


def hidden(mine, got, send=None, share=None):
    rows, units = mine.shape[0] // 2, mine.shape[1]
    shapes = [array(rows, units)]
    args = [mine, got]
    if send is not None:
        shapes.append(array(send.shape[0] + rows, units))
        args.append(send)
    if share is not None:
        shapes.append(array(2 * share.shape[0], units))
        args.append(share)

    def kernel(*refs):
        refs = list(refs)
        mine_ref, got_ref = refs[:2]
        outs = refs[len(args) :]
        activate(mine_ref, got_ref, outs[0])
        if send is not None:
            outs[1][: send.shape[0]] = refs[2][...]
            outs[1][send.shape[0] :] = outs[0][...]
        if share is not None:
            n = share.shape[0]
            outs[-1][:n] = refs[len(args) - 1][...]
            outs[-1][n:] = got_ref[2 * rows : 2 * rows + n]

    return call(kernel, tuple(shapes), tuple(args), "hidden")


def join_kernel(share_ref, got_ref, out_ref):
    n = share_ref.shape[0]
    out_ref[:n] = share_ref[...]
    out_ref[n:] = got_ref[...]


def join(share, got):
    shape = array(2 * share.shape[0], share.shape[1])
    return call(join_kernel, shape, (share, got), "join")


def stack_kernel(first_ref, second_ref, out_ref):
    n = first_ref.shape[0]
    out_ref[:n] = first_ref[...]
    out_ref[n:] = second_ref[...]


def join_rows(first, second):
    shape = array(first.shape[0] + second.shape[0], first.shape[1])
    return call(stack_kernel, shape, (first, second), "stack")


def combine(mine, cores, weight, dtypes):
    rows, columns = 2 * mine.shape[0], weight.shape[1]
    count = len(dtypes)
    piece = rows // WIDTH // count
    shapes = tuple(array(rows // count, columns, dtype) for dtype in dtypes)

    def kernel(mine_ref, *refs):
        core_refs, weight_ref, outs = refs[: len(cores)], refs[len(cores)], refs[-count:]
        core = [ref[...] for ref in core_refs]
        core = jnp.concatenate(core, axis=1) if len(core) > 1 else core[0]
        value = jnp.concatenate([mine_ref[...], core])
        if rows < 128:
            value = jnp.concatenate([value] * (128 // rows))
        for start in range(0, columns, TILE):
            at = slice(start, start + TILE)
            result = dot(value, weight_ref[:, at])
            for p in range(WIDTH):
                for i, out_ref in enumerate(outs):
                    n = (p * count + i) * piece
                    out_ref[p * piece : (p + 1) * piece, at] = result[
                        n : n + piece
                    ].astype(out_ref.dtype)

    return call(kernel, shapes, (mine, *cores, weight), "down")


def join_columns(first, second):
    cut = first.shape[1]

    def kernel(first_ref, second_ref, out_ref):
        out_ref[:, :cut] = first_ref[...]
        out_ref[:, cut:] = second_ref[...]

    shape = array(first.shape[0], cut + second.shape[1])
    return call(kernel, shape, (first, second), "columns")


def combine_parts(mine, cores, weight, dtypes):
    args = (*mine, *cores)
    rows, columns = sum(v.shape[0] for v in args), weight.shape[1]
    count = len(dtypes)
    piece = rows // WIDTH // count
    shapes = tuple(array(rows // count, columns, dtype) for dtype in dtypes)

    def kernel(*refs):
        outs, weight_ref = refs[-count:], refs[len(args)]
        value = jnp.concatenate([ref[...] for ref in refs[: len(args)]])
        if rows < 128:
            value = jnp.concatenate([value] * (128 // rows))
        for start in range(0, columns, TILE):
            at = slice(start, start + TILE)
            result = dot(value, weight_ref[:, at])
            for p in range(WIDTH):
                for i, out_ref in enumerate(outs):
                    n = (p * count + i) * piece
                    out_ref[p * piece : (p + 1) * piece, at] = result[
                        n : n + piece
                    ].astype(out_ref.dtype)

    return call(kernel, shapes, (*args, weight), "down")


def add_kernel(part_ref, got_ref, out_ref):
    out_ref[...] = narrow(part_ref[...] + widen(got_ref[...]))


def peak_kernel(one_ref, other_ref, out_ref):
    out_ref[...] = jnp.maximum(one_ref[...], other_ref[...])


def scale_kernel(first_ref, second_ref, *refs):
    *peak_refs, out_ref, scales_ref = refs
    rows = out_ref.shape[0] // WIDTH
    half = rows // 2
    starts = rows_of(ORDER, lax.axis_index("width"), rows)
    peak = peak_refs[0][...]
    for peak_ref in peak_refs[1:]:
        peak = jnp.maximum(peak, peak_ref[...])
    scales_ref[...] = peak / 448.0
    peak = peak + 1e-06
    for place, start in enumerate(starts):
        here = slice(place * half, (place + 1) * half)
        for offset, ref in ((0, first_ref), (half, second_ref)):
            to = pl.ds(pl.multiple_of(start + offset, half), half)
            out_ref[to] = narrow(ref[here] / peak)


def pipelined(tokens, gate_weight, up_weight, down_weight):
    units = gate_weight.shape[1]
    weights = (gate_weight, up_weight)
    rows = tokens.shape[0]
    stay = rows // 2
    group = stay // 2
    three, two = cuts(2 * units, 3), cuts(2 * units, 2)
    uneven = [0, three[2], 2 * units]
    clock = []

    def ticks(values):
        if clock:
            values = lax.optimization_barrier((*values, *clock))[: len(values)]
            clock[:] = [values[0]]
        return list(values)

    def tick(value):
        return ticks([value])[0]

    def done(values):
        clock.append(values[0] if isinstance(values, (tuple, list)) else values)
        return values

    def parts_of(mine, count):
        bounds = cuts(units, count)
        shapes = [array(mine.shape[0], b - a) for a, b in zip(bounds, bounds[1:])]

        def kernel(mine_ref, *outs):
            for a, b, out_ref in zip(bounds, bounds[1:], outs):
                out_ref[...] = mine_ref[:, a:b]

        return swap_pieces(call(kernel, tuple(shapes), (mine,), "pieces"))

    def arrange(block, cost=SMALL):
        return call(arrange_kernel, array(*block.shape), (block,), "arrange", cost)

    big, wide = rows * tokens.shape[1] * units, gate_weight.size
    near = swap(tokens, AXIS, 1)
    own = arrange(tokens, (8 * big, 4 * wide))
    own_first, own_second = halves(own)
    cross_first = swap(own_first, AXIS, 2)

    keep, *sends = project((own,), weights, [(0, stay, three)], (4 * big, 2 * wide))
    done(keep)
    cores = ticks(swap_pieces(sends))
    mine0, send0 = done(add_cores(keep, cores, group))
    got0 = swap(send0, "width", CORES)

    near = done(arrange(tick(near)))
    keep1, *sends = done(
        project((near,), weights, [(0, group, uneven), (group, group, two)])
    )
    cross_first, *sends = ticks([cross_first, *sends])
    sends5 = sends[2:]
    far_first = swap(cross_first, AXIS, 1)
    cross_second = swap(own_second, AXIS, 2)
    cores = ticks(swap_pieces(sends[:2]))
    mine1, send1 = done(add_cores(keep1, cores, group))

    got0 = tick(got0)
    share0, payload = done(hidden(mine0, got0, send1))
    got1 = swap(payload, "width", CORES)

    cores = ticks(swap_pieces(ticks(sends5)))
    mine5, send5 = done(add_cores(keep1, cores, group, group))

    got1 = tick(got1)
    share1, payload, joined0 = done(hidden(mine1, got1, send5, share0))
    got5 = swap(payload, "width", CORES)
    far_first = done(tick(far_first))
    keep, *sends = done(project((cross_first, far_first), weights, [(0, stay, three)]))
    cross_second, *sends = ticks([cross_second, *sends])
    far_second = swap(cross_second, AXIS, 1)
    cores = ticks(swap_pieces(sends))
    mine2, send2 = done(add_cores(keep, cores, group))

    got5 = tick(got5)
    share5, joined1 = done(hidden(mine5, got5, None, share1))
    got2 = swap(send2, "width", CORES)
    core1 = ticks(parts_of(joined1, 2))
    (part1,) = done(combine(joined1, core1, down_weight, (jnp.bfloat16,)))
    add1 = swap(part1, AXIS, 1)
    far_second = done(tick(far_second))
    keep, *sends = done(
        project((cross_second, far_second), weights, [(0, stay, three)])
    )
    got2, *cores = ticks([got2, *swap_pieces(sends)])

    (share2,) = done(hidden(mine2, got2))
    over2 = swap(share2, "width", CORES)
    early2 = swap(share2, "width", 1)
    mine3, send3, mine4, send4 = done(add_cores(keep, cores, group, split=2))
    payload = done(join_rows(send4, share5))
    core0 = tick(swap(joined0, "width", 1))
    first, second = done(
        combine(joined0, [core0], down_weight, (jnp.float32, jnp.float32))
    )
    got4 = swap(tick(payload), "width", CORES)
    over2, add1, early2 = ticks([over2, add1, early2])
    done(over2)
    core2 = ticks(parts_of(over2, 2))
    cross2, far2 = done(
        combine_parts(
            (share2, over2),
            (early2, done(join_columns(*core2))),
            down_weight,
            (jnp.float32, jnp.bfloat16),
        )
    )
    far2 = swap(far2, AXIS, 1)

    got4 = tick(got4)
    share4, joined5 = done(hidden(mine4, got4, None, share5))
    over4 = swap(share4, "width", CORES)
    early4 = swap(share4, "width", 1)
    over4, early4 = ticks([over4, early4])
    done(over4)
    got3 = swap(tick(send3), "width", CORES)
    core4 = tick(swap(over4, "width", 1))
    (far3,) = done(
        combine_parts((share4, over4), (early4, core4), down_weight, (jnp.bfloat16,))
    )
    far3 = swap(far3, AXIS, 1)
    far2 = tick(far2)
    add2 = done(call(add_kernel, array(stay, tokens.shape[1]), (cross2, far2), "add"))
    add2 = swap(add2, AXIS, 2)
    got3 = tick(got3)
    (share3,) = done(hidden(mine3, got3))
    over3 = swap(share3, "width", CORES)
    early3 = swap(share3, "width", 1)
    core5 = ticks(parts_of(joined5, 2))
    (part5,) = done(combine(joined5, core5, down_weight, (jnp.bfloat16,)))
    add5 = swap(part5, AXIS, 1)
    over3, early3 = ticks([over3, early3])
    done(over3)
    core3 = tick(swap(over3, "width", 1))
    (cross3,) = done(
        combine_parts((share3, over3), (early3, core3), down_weight, (jnp.float32,))
    )
    far3, add2 = ticks([far3, add2])
    add3 = done(call(add_kernel, array(stay, tokens.shape[1]), (cross3, far3), "add"))
    add3 = swap(add3, AXIS, 2)

    first = first + widen(add1) + widen(add2)
    second = second + widen(add5) + widen(add3)
    local_peak = jnp.maximum(
        jnp.max(jnp.abs(first), axis=0, keepdims=True),
        jnp.max(jnp.abs(second), axis=0, keepdims=True),
    )
    pair_peak = call(
        peak_kernel, array(*local_peak.shape, jnp.float32), (local_peak, swap(local_peak, AXIS, 2)), "peak"
    )
    peaks = [swap(pair_peak, AXIS, 1)]
    scaled, scales = call(
        scale_kernel,
        (array(*tokens.shape), array(1, tokens.shape[1], jnp.float32)),
        (first, second, pair_peak, *peaks),
        "scale",
    )
    return (scaled, scales[0])


def plain(tokens, gate_weight, up_weight, down_weight):
    units = gate_weight.shape[1]
    piece = lax.all_gather(tokens, AXIS, axis=0, tiled=True)
    parts = jnp.concatenate([dot(piece, gate_weight), dot(piece, up_weight)], axis=1)
    sums = widen(
        lax.psum_scatter(narrow(parts), "width", scatter_dimension=0, tiled=True)
    )
    share = narrow(jax.nn.silu(sums[:, :units]) * sums[:, units:])
    hidden_units = lax.all_gather(share, "width", axis=0, tiled=True)
    output = widen(
        lax.psum_scatter(
            narrow(dot(hidden_units, down_weight)),
            AXIS,
            scatter_dimension=0,
            tiled=True,
        )
    )
    peak = lax.pmax(jnp.max(jnp.abs(output), axis=0), AXIS)
    return (narrow(output / (peak + 1e-06)), peak / 448.0)


def solution(mesh):
    in_specs = (
        P(("groups", "tensor"), "width"),
        P("width", "tensor"),
        P("width", "tensor"),
        P("tensor", "width"),
    )
    out_specs = (P(("groups", "tensor"), "width"), P(("groups", "width")))
    fits = mesh.shape[AXIS] == RANKS and mesh.shape["width"] == WIDTH
    return jax.shard_map(
        pipelined if fits else plain,
        mesh=mesh,
        in_specs=in_specs,
        out_specs=out_specs,
        check_vma=False,
    )
```
